32 devices in a mesh: seg: 2 (over y), chan: 16 (over z, x, core).
Axes of the slice: x: 2, y: 2, z: 4, core: 2. Of those that a mesh axis runs over, the one named last changes fastest.
Arguments:
- traces: bfloat16 [2, 1024, 4096], P('seg', 'chan'), may hold values from -60 to 60
- partners: int32 [16, 11], P('chan'), may hold values from -1 to 15, as said below
Outputs:
- stacked: float32 [16, 11, 65, 4096], P('chan', None, None, 'seg')
The draws below stay inside these ranges and needn't reach their ends.
Inputs may be any that keep to these rules, and one draw needn't show every extreme that they name: `partners`: entry q of block i is i + q - 5 if blocks i and i + q - 5 form a pair and -1 otherwise. Entry 5 is always i. The list is symmetric: j stands in the row of i exactly when i stands in the row of j.
All inputs are finite; a program needn't handle non-finite values.
Results may differ from the reference program's by a relative error of at most 0.013.
Values may be sent and summed in bfloat16 or wider, within the bound.
No kernel may reach another device: no remote copies, remote signals or barrier semaphores. Data moves between devices by JAX's collectives and lax.ppermute only.
A program may use at most 128 MiB of HBM per device.

```python
import math
import jax
import jax.numpy as jnp
from jax import lax

CHB = 64
SAMPLES = 4096
BAND = 256
BAND_LO = 16
REACH = 5
LAGS = 65
CAP = 11
NB = 16
NCH = 1024
NSEG = 2


def draw_traces(key, part):
    key_scale, key_base = jax.random.split(key, 2)
    amplitude = jnp.exp(jax.random.uniform(key_scale, (NSEG, NCH, 1), jnp.float32, 0.0, math.log(10.0)))
    signal = jnp.clip(jax.random.normal(key_base, (NSEG, NCH, SAMPLES), jnp.float32), -6.0, 6.0)
    return (signal * amplitude).astype(jnp.bfloat16)


def draw_partners(key, part):
    keeps = jax.random.randint(key, (NB, REACH), 0, 10, dtype=jnp.int32) < 7
    blocks = jnp.arange(NB, dtype=jnp.int32)
    entries = []
    for slot in range(2 * REACH + 1):
        offset = slot - REACH
        if offset == 0:
            entries.append(blocks)
        elif offset < 0:
            distance = -offset
            kept = jnp.roll(keeps[:, distance - 1], distance)
            live = kept & (blocks >= distance)
            entries.append(jnp.where(live, blocks + offset, -1))
        else:
            live = keeps[:, offset - 1] & (blocks + offset < NB)
            entries.append(jnp.where(live, blocks + offset, -1))
    return jnp.stack(entries, axis=1).astype(jnp.int32)


def setup_inputs(seed: int = 0) -> dict:
    streams_of = jax.random.split(jax.random.key(seed), 3)
    traces = draw_traces(jax.random.fold_in(streams_of[2], 71), 0)
    partners = draw_partners(jax.random.fold_in(streams_of[2], 71), 0)
    return dict(traces=traces, partners=partners)


full_turn = 2.0 * math.pi
water_level = 0.5
epsilon = 1e-06

def lag_tables(band_bins, band_low, lag_count, samples):
    lag_half = (lag_count - 1) // 2
    bins = jnp.arange(band_bins, dtype=jnp.int32) + band_low
    shifts = jnp.arange(lag_count, dtype=jnp.int32) - lag_half
    phase = jnp.mod(shifts[:, None] * bins[None, :], samples)
    angle = phase.astype(jnp.float32) * (full_turn / samples)
    return (jnp.cos(angle), jnp.sin(angle))

def whiten(real_part, imag_part):
    power = real_part * real_part + imag_part * imag_part
    level = lax.optimization_barrier(jnp.mean(power, axis=-1, keepdims=True))
    denom = jnp.sqrt(power + water_level * level + epsilon)
    return jnp.concatenate([real_part / denom, imag_part / denom], axis=-1).astype(jnp.bfloat16)

def lagged(spectra, cos_table, sin_table):
    band_bins = cos_table.shape[1]
    lag_count = cos_table.shape[0]
    real_part = spectra[..., :band_bins].astype(jnp.float32)[None]
    imag_part = spectra[..., band_bins:].astype(jnp.float32)[None]
    cosine = cos_table[:, None, None, :]
    sine = sin_table[:, None, None, :]
    turned = jnp.concatenate([real_part * cosine - imag_part * sine, real_part * sine + imag_part * cosine], axis=-1)
    return turned.reshape(lag_count * spectra.shape[0], spectra.shape[1] * 2 * band_bins).astype(jnp.bfloat16)

def columns(window):
    moved = jnp.transpose(window, (0, 3, 1, 2))
    return moved.reshape(window.shape[0] * window.shape[3], window.shape[1] * window.shape[2])

def tile_block(lagged_rows, partner_columns, live_pairs, rows_a, norm_scale):
    product = jnp.dot(lagged_rows, partner_columns, preferred_element_type=jnp.float32)
    slots = live_pairs.shape[0]
    lag_count = product.shape[0] // rows_a
    width = product.shape[1] // slots
    product = product.reshape(lag_count, rows_a, slots, width).transpose(2, 0, 1, 3)
    product = product.reshape(slots, lag_count, rows_a * width)
    return product * norm_scale * live_pairs[:, None, None]

def reference(traces, partners):
    signal = traces.astype(jnp.float32)
    spectrum = jnp.fft.rfft(signal, axis=-1)[..., BAND_LO:BAND_LO + BAND]
    white = whiten(jnp.real(spectrum), jnp.imag(spectrum))
    blocks = white.reshape(NSEG, NB, CHB, 2 * BAND)
    padded = jnp.pad(blocks, ((0, 0), (REACH, REACH), (0, 0), (0, 0)))
    cos_table, sin_table = lag_tables(BAND, BAND_LO, LAGS, SAMPLES)
    norm_scale = (NSEG * BAND) ** (-0.5)

    def one_block(index):
        window = lax.dynamic_slice_in_dim(padded, index, CAP, 1)
        own_block = lax.dynamic_slice_in_dim(blocks, index, 1, 1)[:, 0]
        rows = lagged(jnp.transpose(own_block, (1, 0, 2)), cos_table, sin_table)
        pair_row = lax.dynamic_index_in_dim(partners, index, 0, keepdims=False)
        live_pairs = (pair_row >= 0).astype(jnp.float32)
        return tile_block(rows, columns(window), live_pairs, CHB, norm_scale)
    return lax.map(one_block, jnp.arange(NB, dtype=jnp.int32))
```

```python
import functools
import math

import jax
import jax.numpy as jnp
import numpy as np
from jax import lax
from jax.experimental import pallas as pl
from jax.experimental.pallas import tpu as pltpu
from jax.sharding import PartitionSpec as P

BAND = 256
BAND_LO = 16
LAG = 32
LAGS = 2 * LAG + 1
LAG_ROWS = 72
QUAD = 4

water_level = 0.5
epsilon = 1e-06


def split_table(samples, step):
    bins = np.arange(BAND) + BAND_LO
    angle = (np.arange(step)[:, None] * bins[None, :] % samples) * (2.0 * math.pi / samples)
    table = np.concatenate([np.cos(angle), -np.sin(angle)], axis=1).astype(np.float32)
    high = table.astype(jnp.bfloat16)
    low = (table - high.astype(np.float32)).astype(jnp.bfloat16)
    stretches = samples // step
    turn = (np.arange(stretches)[:, None] * step * bins[None, :] % samples) * (2.0 * math.pi / samples)
    return high, low, np.cos(turn).astype(np.float32), np.sin(turn).astype(np.float32)


def lag_tables(samples):
    bins = np.arange(BAND) + BAND_LO
    shifts = np.arange(LAG_ROWS) - LAG
    angle = (shifts[:, None] * bins[None, :] % samples) * (2.0 * math.pi / samples)
    return np.cos(angle).astype(np.float32), np.sin(angle).astype(np.float32)


def spectrum_kernel(step, traces_ref, high_ref, low_ref, cos_ref, sin_ref, white_ref):
    stretches = traces_ref.shape[1] // step
    real = imag = None
    for stretch in range(stretches):
        part = traces_ref[:, stretch * step : (stretch + 1) * step]
        y = jnp.dot(part, high_ref[...], preferred_element_type=jnp.float32)
        y = y + jnp.dot(part, low_ref[...], preferred_element_type=jnp.float32)
        y_real, y_imag = y[:, :BAND], y[:, BAND:]
        if stretch == 0:
            real, imag = y_real, y_imag
            continue
        cosine = cos_ref[stretch : stretch + 1, :]
        sine = sin_ref[stretch : stretch + 1, :]
        real = real + (y_real * cosine + y_imag * sine)
        imag = imag + (y_imag * cosine - y_real * sine)
    power = real * real + imag * imag
    level = jnp.mean(power, axis=1, keepdims=True)
    denom = jnp.sqrt(power + water_level * level + epsilon)
    white_ref[:, :BAND] = (real / denom).astype(jnp.bfloat16)
    white_ref[:, BAND:] = (imag / denom).astype(jnp.bfloat16)


def spectra(traces):
    channels, samples = traces.shape
    step = 256
    tables = split_table(samples, step)
    return pl.pallas_call(
        functools.partial(spectrum_kernel, step),
        out_shape=jax.ShapeDtypeStruct((channels, 2 * BAND), jnp.bfloat16),
        compiler_params=pltpu.CompilerParams(vmem_limit_bytes=32 * 2**20),
    )(traces, *(jnp.asarray(t) for t in tables))


def stack_kernel(norm_scale, place_ref, live_ref, own_ref, cos_ref, sin_ref, blobs_ref, out_ref,
                 own, rows, window, tiles, in_sems, out_sems):
    slots = live_ref.shape[1]
    width = window.shape[1]
    half = own.shape[0]
    pairs = half // 2
    pair_rows = 2 * LAG_ROWS
    copies = [
        pltpu.make_async_copy(blobs_ref.at[place_ref[slot]], window.at[slot], in_sems.at[slot])
        for slot in range(slots)
    ]
    for copy in copies:
        copy.start()
    first = pl.multiple_of(place_ref[slots], half)
    own[...] = own_ref[pl.ds(first, half), :].astype(jnp.float32)

    def turn(pair, carry):
        for part in range(own.shape[1] // (2 * BAND)):
            left = part * 2 * BAND
            reals, imags = [], []
            for member in range(2):
                real = own[pl.ds(pair * 2 + member, 1), left : left + BAND]
                imag = own[pl.ds(pair * 2 + member, 1), left + BAND : left + 2 * BAND]
                reals.append(real * cos_ref[...] - imag * sin_ref[...])
                imags.append(real * sin_ref[...] + imag * cos_ref[...])
            at = pl.ds(pl.multiple_of(pair * pair_rows, pair_rows), pair_rows)
            rows[at, left : left + BAND] = jnp.concatenate(reals, axis=0).astype(jnp.bfloat16)
            rows[at, left + BAND : left + 2 * BAND] = jnp.concatenate(imags, axis=0).astype(jnp.bfloat16)
        return carry

    lax.fori_loop(0, pairs, turn, 0)
    group = 4
    chunk = 4
    sent = []
    for number, start in enumerate(range(0, slots, group)):
        members = list(range(start, min(start + group, slots)))
        buffer = number % 2
        for slot in members:
            copies[slot].wait()
        if number >= 2:
            for copy in sent[number - 2]:
                copy.wait()
        partner = window[start : start + len(members)].reshape(len(members) * width, window.shape[2])
        scales = [jnp.where(live_ref[0, slot] >= 0, norm_scale, 0.0) for slot in members]

        def multiply(step, carry):
            at = pl.multiple_of(step * chunk * pair_rows, chunk * pair_rows)
            product = lax.dot_general(
                rows[pl.ds(at, chunk * pair_rows), :], partner, (((1,), (1,)), ((), ())),
                preferred_element_type=jnp.float32,
            )
            lane = lax.broadcasted_iota(jnp.int32, (LAG_ROWS, 2 * width), 1)
            for inner in range(chunk):
                lanes = pl.ds(pl.multiple_of((step * chunk + inner) * 2 * width, 2 * width), 2 * width)
                even = product[inner * pair_rows : inner * pair_rows + LAG_ROWS]
                odd = product[inner * pair_rows + LAG_ROWS : (inner + 1) * pair_rows]
                for place in range(0, len(members), 2):
                    both = min(2, len(members) - place)
                    a = even[:, place * width : (place + both) * width]
                    b = odd[:, place * width : (place + both) * width]
                    if both == 1:
                        tiles[buffer, place, :, lanes] = (jnp.concatenate([a, b], axis=1) * scales[place])[:LAGS]
                        continue
                    a_far, b_far = pltpu.roll(a, width, 1), pltpu.roll(b, width, 1)
                    tiles[buffer, place, :, lanes] = (jnp.where(lane < width, a, b_far) * scales[place])[:LAGS]
                    tiles[buffer, place + 1, :, lanes] = (jnp.where(lane < width, a_far, b) * scales[place + 1])[:LAGS]
            return carry

        lax.fori_loop(0, pairs // chunk, multiply, 0)
        out = [
            pltpu.make_async_copy(
                tiles.at[buffer, place], out_ref.at[slot], out_sems.at[buffer, place]
            )
            for place, slot in enumerate(members)
        ]
        for copy in out:
            copy.start()
        sent.append(out)
    for out in sent[-2:]:
        for copy in out:
            copy.wait()


def correlate(own, blobs, place, live, samples, half, norm_scale):
    slots = live.shape[1]
    width, depth = blobs.shape[1:]
    cosine, sine = lag_tables(samples)
    smem = pl.BlockSpec(memory_space=pltpu.SMEM)
    vmem = pl.BlockSpec(memory_space=pltpu.VMEM)
    anywhere = pl.BlockSpec(memory_space=pl.ANY)
    return pl.pallas_call(
        functools.partial(stack_kernel, norm_scale),
        out_shape=jax.ShapeDtypeStruct((slots, LAGS, half * width), jnp.float32),
        in_specs=[smem, smem, vmem, vmem, vmem, anywhere],
        out_specs=anywhere,
        scratch_shapes=[
            pltpu.VMEM((half, depth), jnp.float32),
            pltpu.VMEM((half * LAG_ROWS, depth), jnp.bfloat16),
            pltpu.VMEM((slots, width, depth), jnp.bfloat16),
            pltpu.VMEM((2, 4, LAGS, half * width), jnp.float32),
            pltpu.SemaphoreType.DMA((slots,)),
            pltpu.SemaphoreType.DMA((2, 4)),
        ],
        compiler_params=pltpu.CompilerParams(vmem_limit_bytes=48 * 2**20),
        cost_estimate=pl.CostEstimate(
            flops=2 * half * LAGS * depth * slots * width, bytes_accessed=8 * 2**20, transcendentals=0
        ),
    )(place, live, own, jnp.asarray(cosine), jnp.asarray(sine), blobs)


def places(reach):
    table = np.zeros((QUAD, 2 * reach + 1), np.int32)
    for position in range(QUAD):
        for slot in range(2 * reach + 1):
            other = position + slot - reach
            plane = other // QUAD
            if abs(plane) > 1:
                table[position, slot] = 12
                continue
            swap = (other % QUAD) ^ position
            table[position, slot] = 6 * (swap % 2) + 2 * (plane % 3) + swap // 2
    return table


def local(traces, partners):
    samples = traces.shape[2]
    slots = partners.shape[1]
    reach = (slots - 1) // 2
    segments = lax.axis_size("seg")
    blocks = lax.axis_size("chan")
    half = traces.shape[1] // segments
    assert segments == 2 and blocks % QUAD == 0 and reach == QUAD + 1
    swap = lambda by: [(i, i ^ by) for i in range(blocks)]
    shift = lambda by: [(i, i + by) for i in range(blocks) if 0 <= i + by < blocks]
    far = QUAD + 1
    corners = [(i, i + far) for i in range(QUAD - 1, blocks - far, QUAD)]
    corners += [(i, i - far) for i in range(2 * QUAD, blocks, QUAD)]

    white = spectra(traces[0])
    other = lax.ppermute(white, "seg", [(0, 1), (1, 0)])
    pair = jnp.concatenate([white, other], axis=1)
    quad = jnp.stack([pair, lax.ppermute(pair, "chan", swap(2))])
    corner = lax.ppermute(pair, "chan", corners)
    after = lax.ppermute(quad, "chan", shift(-QUAD))
    before = lax.ppermute(quad, "chan", shift(QUAD))
    mine = jnp.concatenate([quad, after, before], axis=0)
    sibling = lax.ppermute(mine, "chan", swap(1))
    blobs = jnp.concatenate([mine, sibling, corner[None]], axis=0)

    index = lax.axis_index("chan")
    place = jnp.asarray(places(reach))[index % QUAD]
    first = (lax.axis_index("seg") * half).astype(jnp.int32)
    place = jnp.concatenate([place, first[None]])
    norm_scale = (segments * BAND) ** (-0.5)
    return correlate(pair, blobs, place, partners, samples, half, norm_scale)[None]


def solution(mesh):
    placed = (P("seg", "chan", None), P("chan", None))
    return jax.shard_map(
        local, mesh=mesh, in_specs=placed, out_specs=P("chan", None, None, "seg"), check_vma=False
    )
```

```python
import functools
import math

import jax
import jax.numpy as jnp
import numpy as np
from jax import lax
from jax.experimental import pallas as pl
from jax.experimental.pallas import tpu as pltpu
from jax.sharding import PartitionSpec as P

BAND = 256
BAND_LO = 16
LAG = 32
LAGS = 2 * LAG + 1
REACH = 5
QUAD = 4
SPECTRUM_VMEM = 56 * 2**20
KERNEL_VMEM = 24 * 2**20

water_level = 0.5
epsilon = 1e-06


def split_table(samples, step):
    bins = np.arange(BAND) + BAND_LO
    angle = (np.arange(step)[:, None] * bins[None, :] % samples) * (2.0 * math.pi / samples)
    table = np.concatenate([np.cos(angle), -np.sin(angle)], axis=1).astype(np.float32)
    high = table.astype(jnp.bfloat16)
    low = (table - high.astype(np.float32)).astype(jnp.bfloat16)
    stretches = samples // step
    turn = (np.arange(stretches)[:, None] * step * bins[None, :] % samples) * (2.0 * math.pi / samples)
    return high, low, np.cos(turn).astype(np.float32), np.sin(turn).astype(np.float32)


def lag_tables(samples):
    bins = np.arange(BAND) + BAND_LO
    shifts = np.arange(LAGS) - LAG
    angle = (shifts[:, None] * bins[None, :] % samples) * (2.0 * math.pi / samples)
    return np.stack([np.cos(angle), np.sin(angle)]).astype(np.float32)


def spectrum_kernel(step, traces_hbm, table_hbm, turn_hbm, white_ref, traces, table, turn, sems):
    copies = [
        pltpu.make_async_copy(table_hbm, table, sems.at[0]),
        pltpu.make_async_copy(traces_hbm, traces, sems.at[1]),
        pltpu.make_async_copy(turn_hbm, turn, sems.at[2]),
    ]
    for copy in copies:
        copy.start()
    for copy in copies:
        copy.wait()
    real = imag = None
    for stretch in range(traces.shape[1] // step):
        part = traces[:, stretch * step : (stretch + 1) * step]
        y = jnp.dot(part, table[0], preferred_element_type=jnp.float32)
        y = y + jnp.dot(part, table[1], preferred_element_type=jnp.float32)
        y_real, y_imag = y[:, :BAND], y[:, BAND:]
        if stretch == 0:
            real, imag = y_real, y_imag
            continue
        cosine = turn[0, stretch : stretch + 1, :]
        sine = turn[1, stretch : stretch + 1, :]
        real = real + (y_real * cosine + y_imag * sine)
        imag = imag + (y_imag * cosine - y_real * sine)
    power = real * real + imag * imag
    level = jnp.mean(power, axis=1, keepdims=True)
    denom = jnp.sqrt(power + water_level * level + epsilon)
    white_ref[:, :BAND] = (real / denom).astype(jnp.bfloat16)
    white_ref[:, BAND:] = (imag / denom).astype(jnp.bfloat16)


def spectra(traces):
    channels, samples = traces.shape
    step = 256
    high, low, cosine, sine = split_table(samples, step)
    table, turn = np.stack([high, low]), np.stack([cosine, sine])
    anywhere = pl.BlockSpec(memory_space=pl.ANY)
    return pl.pallas_call(
        functools.partial(spectrum_kernel, step),
        out_shape=jax.ShapeDtypeStruct((channels, 2 * BAND), jnp.bfloat16),
        in_specs=[anywhere] * 3,
        out_specs=pl.BlockSpec(memory_space=pltpu.VMEM),
        scratch_shapes=[
            pltpu.VMEM(traces.shape, traces.dtype),
            pltpu.VMEM(table.shape, jnp.bfloat16),
            pltpu.VMEM(turn.shape, jnp.float32),
            pltpu.SemaphoreType.DMA((3,)),
        ],
        compiler_params=pltpu.CompilerParams(vmem_limit_bytes=SPECTRUM_VMEM),
    )(traces, jnp.asarray(table), jnp.asarray(turn))


def rows_kernel(pair_ref, lag_ref, rows_ref, stage, own):
    pairs = own.shape[1]
    first = pl.multiple_of(lax.axis_index("seg") * 2 * pairs, 2 * pairs)
    mine = pair_ref[pl.ds(first, 2 * pairs), :].astype(jnp.float32)
    for left in range(0, mine.shape[1], 128):
        stage[...] = mine[:, left : left + 128]
        for member in range(2):
            own[member, :, left : left + 128] = stage[pl.ds(member, pairs, stride=2), :]

    def turn(lag, carry):
        cosine = lag_ref[0, pl.ds(lag, 1), :]
        sine = lag_ref[1, pl.ds(lag, 1), :]
        at = pl.ds(pl.multiple_of(lag * pairs, pairs), pairs)
        for member in range(2):
            for left in range(0, own.shape[2], 2 * BAND):
                middle, right = left + BAND, left + 2 * BAND
                real, imag = own[member, :, left:middle], own[member, :, middle:right]
                rows_ref[member, at, left:middle] = (real * cosine - imag * sine).astype(jnp.bfloat16)
                rows_ref[member, at, middle:right] = (real * sine + imag * cosine).astype(jnp.bfloat16)
        return carry

    lax.fori_loop(0, LAGS, turn, 0, unroll=5)


def lag_rows(pair, samples, half):
    depth = pair.shape[1]
    vmem = pl.BlockSpec(memory_space=pltpu.VMEM)
    return pl.pallas_call(
        rows_kernel,
        out_shape=jax.ShapeDtypeStruct((2, LAGS * half // 2, depth), jnp.bfloat16),
        in_specs=[vmem] * 2,
        out_specs=vmem,
        scratch_shapes=[pltpu.VMEM((half, 128), jnp.float32), pltpu.VMEM((2, half // 2, depth), jnp.float32)],
        compiler_params=pltpu.CompilerParams(vmem_limit_bytes=KERNEL_VMEM),
        cost_estimate=pl.CostEstimate(flops=6 * half * LAGS * depth, bytes_accessed=2**20, transcendentals=0),
    )(pair, jnp.asarray(lag_tables(samples)))


def multiply(rows, partner, scale, tile):
    members = len(scale)
    width = partner.shape[0] // members
    even, odd = [
        lax.dot_general(rows[m], partner, (((1,), (1,)), ((), ())), preferred_element_type=jnp.float32)
        for m in range(2)
    ]
    lane = lax.broadcasted_iota(jnp.int32, (even.shape[0], 2 * width), 1)
    for n in range(0, members, 2):
        a, b = even[:, n * width : (n + 2) * width], odd[:, n * width : (n + 2) * width]
        if n + 1 == members:
            tile[n][...] = jnp.concatenate([a, b], axis=1) * scale[n]
            continue
        tile[n][...] = jnp.where(lane < width, a, pltpu.roll(b, width, 1)) * scale[n]
        tile[n + 1][...] = jnp.where(lane < width, pltpu.roll(a, width, 1), b) * scale[n + 1]


def position():
    place = lax.rem(lax.axis_index("chan"), QUAD)
    return place, REACH - place


def slot_of(place, plane, swap_x, swap_core):
    step_x = 2 - 4 * lax.div(place, 2)
    step_core = 1 - 2 * lax.rem(place, 2)
    return REACH + QUAD * plane + swap_x * step_x + swap_core * step_core


def near_kernel(rows_ref, scale_ref, quad_ref, sibling_ref, out_ref, window, tiles, sems):
    place, _ = position()
    width = quad_ref.shape[1]
    for core, ref in enumerate((quad_ref, sibling_ref)):
        for x in range(2):
            n = 2 * core + x
            window[n * width : (n + 1) * width] = ref[x]
    slots = [slot_of(place, 0, n % 2, n // 2) for n in range(QUAD)]
    scale = [scale_ref[pl.ds(slot, 1), :] for slot in slots]
    multiply([rows_ref[0], rows_ref[1]], window[...], scale, [tiles.at[n] for n in range(QUAD)])
    copies = [
        pltpu.make_async_copy(tiles.at[n], out_ref.at[slot], sems.at[n]) for n, slot in enumerate(slots)
    ]
    for copy in copies:
        copy.start()
    for copy in copies:
        copy.wait()


def far_kernel(rows_ref, scale_ref, after_ref, before_ref, sib_after_ref, sib_before_ref, corner_ref, near_ref,
               out_ref, window, tiles, sems):
    del near_ref
    place, first = position()
    width = corner_ref.shape[0]
    total = tiles.shape[0]

    def put(slot, valid, value):
        at = jnp.where(slot < first, slot, slot - QUAD)

        @pl.when(valid)
        def _():
            window[pl.ds(pl.multiple_of(at * width, width), width), :] = value()

    blobs = ((after_ref, 1, 0), (before_ref, -1, 0), (sib_after_ref, 1, 1), (sib_before_ref, -1, 1))
    for ref, plane, core in blobs:
        for x in range(2):
            slot = slot_of(place, plane, x, core)
            put(slot, (slot >= 0) & (slot <= 2 * REACH), lambda ref=ref, x=x: ref[x])
    put(jnp.where(place == 0, 0, 2 * REACH), (place == 0) | (place == QUAD - 1), lambda: corner_ref[...])

    copies = []
    for start in range(0, total, QUAD):
        members = range(start, min(start + QUAD, total))
        slots = [jnp.where(n < first, n, n + QUAD) for n in members]
        scale = [scale_ref[pl.ds(slot, 1), :] for slot in slots]
        partner = window[start * width : (start + len(members)) * width]
        multiply([rows_ref[0], rows_ref[1]], partner, scale, [tiles.at[n] for n in members])
        for n, slot in zip(members, slots):
            copy = pltpu.make_async_copy(tiles.at[n], out_ref.at[slot], sems.at[n])
            copy.start()
            copies.append(copy)
    for copy in copies:
        copy.wait()


def correlate(kernel, rows, scale, blobs, out, count):
    width, depth = blobs[0].shape[-2:]
    lines = rows.shape[1]
    vmem = pl.BlockSpec(memory_space=pltpu.VMEM)
    anywhere = pl.BlockSpec(memory_space=pl.ANY)
    extra = [] if out is None else [out]
    operands = [rows, scale, *blobs, *extra]
    return pl.pallas_call(
        kernel,
        out_shape=jax.ShapeDtypeStruct((scale.shape[0], lines, 2 * width), jnp.float32),
        in_specs=[vmem] * (2 + len(blobs)) + [anywhere] * len(extra),
        out_specs=anywhere,
        scratch_shapes=[
            pltpu.VMEM((count * width, depth), jnp.bfloat16),
            pltpu.VMEM((count, lines, 2 * width), jnp.float32),
            pltpu.SemaphoreType.DMA((count,)),
        ],
        input_output_aliases={len(operands) - 1: 0} if extra else {},
        compiler_params=pltpu.CompilerParams(vmem_limit_bytes=KERNEL_VMEM),
        cost_estimate=pl.CostEstimate(
            flops=4 * lines * depth * count * width, bytes_accessed=8 * count * lines * width, transcendentals=0
        ),
    )(*operands)


def local(traces, partners):
    samples = traces.shape[2]
    slots = partners.shape[1]
    segments = lax.axis_size("seg")
    blocks = lax.axis_size("chan")
    channels = traces.shape[1]
    half = channels // segments
    assert segments == 2 and blocks % QUAD == 0 and slots == 2 * REACH + 1
    swap = lambda by: [(i, i ^ by) for i in range(blocks)]
    shift = lambda by: [(i, i + by) for i in range(blocks) if 0 <= i + by < blocks]
    corners = [(i, i + REACH) for i in range(QUAD - 1, blocks - REACH, QUAD)]
    corners += [(i, i - REACH) for i in range(2 * QUAD, blocks, QUAD)]
    norm_scale = (segments * BAND) ** (-0.5)
    scale = jnp.where(partners[0] >= 0, norm_scale, 0.0).astype(jnp.float32)
    scale = jnp.broadcast_to(scale[:, None], (slots, 2 * channels))

    white = spectra(traces[0])
    other = lax.ppermute(white, "seg", [(0, 1), (1, 0)])
    pair = jnp.concatenate([white, other], axis=1)
    rows = lag_rows(pair, samples, half)
    quad = jnp.stack([pair, lax.ppermute(pair, "chan", swap(2))])
    corner = lax.ppermute(pair, "chan", corners)
    after = lax.ppermute(quad, "chan", shift(-QUAD))
    before = lax.ppermute(quad, "chan", shift(QUAD))
    out = correlate(near_kernel, rows, scale, [quad, lax.ppermute(quad, "chan", swap(1))], None, QUAD)
    sib_after = lax.ppermute(after, "chan", swap(1))
    sib_before = lax.ppermute(before, "chan", swap(1))
    blobs = [after, before, sib_after, sib_before, corner]
    out = correlate(far_kernel, rows, scale, blobs, out, slots - QUAD)
    return out.reshape(1, slots, LAGS, half * channels)


def solution(mesh):
    placed = (P("seg", "chan", None), P("chan", None))
    return jax.shard_map(
        local, mesh=mesh, in_specs=placed, out_specs=P("chan", None, None, "seg"), check_vma=False
    )
```

```python
import functools
import math

import jax
import jax.numpy as jnp
import numpy as np
from jax import lax
from jax.experimental import pallas as pl
from jax.experimental.pallas import tpu as pltpu
from jax.sharding import PartitionSpec as P

BAND = 256
BAND_LO = 16
LAG = 32
LAGS = 2 * LAG + 1
REACH = 5
QUAD = 4
SPECTRUM_VMEM = 55040 * 2**10
KERNEL_VMEM = 24 * 2**20

water_level = 0.5
epsilon = 1e-06


def split_table(samples, step):
    bins = np.arange(BAND) + BAND_LO
    angle = (np.arange(step)[:, None] * bins[None, :] % samples) * (2.0 * math.pi / samples)
    table = np.concatenate([np.cos(angle), -np.sin(angle)], axis=1).astype(np.float32)
    high = table.astype(jnp.bfloat16)
    low = (table - high.astype(np.float32)).astype(jnp.bfloat16)
    return np.stack([high, low])


def spectrum_kernel(step, traces_hbm, table_hbm, white_ref, traces, table, sems):
    channels = white_ref.shape[0]
    stretches = traces.shape[0] // channels
    group = 4
    table_copy = pltpu.make_async_copy(table_hbm, table, sems.at[stretches])
    table_copy.start()
    copies = [
        pltpu.make_async_copy(
            traces_hbm.at[:, pl.ds(n * step, step)], traces.at[pl.ds(n * channels, channels)], sems.at[n]
        )
        for n in range(stretches)
    ]
    for copy in copies:
        copy.start()
    number = lax.broadcasted_iota(jnp.int32, (stretches, BAND), 0)
    bins = lax.broadcasted_iota(jnp.int32, (stretches, BAND), 1) + BAND_LO
    turn = lax.rem(number * bins, stretches).astype(jnp.float32) * (2.0 * math.pi / stretches)
    turn_cos, turn_sin = jnp.cos(turn), jnp.sin(turn)
    table_copy.wait()
    real = imag = None
    for start in range(0, stretches, group):
        for copy in copies[start : start + group]:
            copy.wait()
        part = traces[start * channels : (start + group) * channels]
        y = jnp.dot(part, table[0], preferred_element_type=jnp.float32)
        y = y + jnp.dot(part, table[1], preferred_element_type=jnp.float32)
        for n in range(group):
            y_real = y[n * channels : (n + 1) * channels, :BAND]
            y_imag = y[n * channels : (n + 1) * channels, BAND:]
            if start + n == 0:
                real, imag = y_real, y_imag
                continue
            cosine, sine = turn_cos[start + n : start + n + 1], turn_sin[start + n : start + n + 1]
            real = real + (y_real * cosine + y_imag * sine)
            imag = imag + (y_imag * cosine - y_real * sine)
    power = real * real + imag * imag
    level = jnp.mean(power, axis=1, keepdims=True)
    denom = jnp.sqrt(power + water_level * level + epsilon)
    white_ref[:, :BAND] = (real / denom).astype(jnp.bfloat16)
    white_ref[:, BAND:] = (imag / denom).astype(jnp.bfloat16)


def spectra(traces):
    channels, samples = traces.shape
    step = 256
    table = split_table(samples, step)
    hbm = pl.BlockSpec(memory_space=pltpu.HBM)
    return pl.pallas_call(
        functools.partial(spectrum_kernel, step),
        out_shape=jax.ShapeDtypeStruct((channels, 2 * BAND), jnp.bfloat16),
        in_specs=[hbm] * 2,
        out_specs=pl.BlockSpec(memory_space=pltpu.VMEM),
        scratch_shapes=[
            pltpu.VMEM((samples // step * channels, step), traces.dtype),
            pltpu.VMEM(table.shape, jnp.bfloat16),
            pltpu.SemaphoreType.DMA((samples // step + 1,)),
        ],
        compiler_params=pltpu.CompilerParams(vmem_limit_bytes=SPECTRUM_VMEM),
    )(traces, jnp.asarray(table))


def turn_rows(samples, pair_ref, rows_ref, stage, own, lag_cos, lag_sin):
    lag = lax.broadcasted_iota(jnp.int32, lag_cos.shape, 0)
    bins = lax.broadcasted_iota(jnp.int32, lag_cos.shape, 1) + BAND_LO
    angle = lax.rem((lag + (samples - LAG)) * bins, samples).astype(jnp.float32) * (2.0 * math.pi / samples)
    lag_cos[...] = jnp.cos(angle)
    lag_sin[...] = jnp.sin(angle)
    pairs = own.shape[1]
    first = pl.multiple_of(lax.axis_index("seg") * 2 * pairs, 2 * pairs)
    mine = pair_ref[0, pl.ds(first, 2 * pairs), :].astype(jnp.float32)
    for left in range(0, mine.shape[1], 128):
        stage[...] = mine[:, left : left + 128]
        for member in range(2):
            own[member, :, left : left + 128] = stage[pl.ds(member, pairs, stride=2), :]

    def turn(lag, carry):
        cosine, sine = lag_cos[pl.ds(lag, 1), :], lag_sin[pl.ds(lag, 1), :]
        at = pl.ds(pl.multiple_of(lag * pairs, pairs), pairs)
        for member in range(2):
            for left in range(0, own.shape[2], 2 * BAND):
                middle, right = left + BAND, left + 2 * BAND
                real, imag = own[member, :, left:middle], own[member, :, middle:right]
                rows_ref[member, at, left:middle] = (real * cosine - imag * sine).astype(jnp.bfloat16)
                rows_ref[member, at, middle:right] = (real * sine + imag * cosine).astype(jnp.bfloat16)
        return carry

    lax.fori_loop(0, LAGS, turn, 0, unroll=5)


def multiply(rows_ref, window, scale, tiles, done):
    members = len(scale)
    width = window.shape[0] // members
    lines = rows_ref.shape[1]
    bounds = [lines * cut // 13 // 16 * 16 for cut in (0, 6, 10)] + [lines]
    for number, (low, high) in enumerate(zip(bounds[:-1], bounds[1:])):
        even, odd = [
            lax.dot_general(
                rows_ref[m, low:high], window[...], (((1,), (1,)), ((), ())), preferred_element_type=jnp.float32
            )
            for m in range(2)
        ]
        lane = lax.broadcasted_iota(jnp.int32, (high - low, 2 * width), 1)
        for n in range(0, members, 2):
            a, b = even[:, n * width : (n + 2) * width], odd[:, n * width : (n + 2) * width]
            tiles[n, low:high] = jnp.where(lane < width, a, pltpu.roll(b, width, 1)) * scale[n]
            tiles[n + 1, low:high] = jnp.where(lane < width, pltpu.roll(a, width, 1), b) * scale[n + 1]
        done(number, low, high)


class Sender:
    def __init__(self, tiles, slots, out_ref, sems, checked):
        self.tiles, self.slots, self.out_ref, self.sems, self.checked = tiles, slots, out_ref, sems, checked
        self.sent = []

    def act(self, slot, action):
        if self.checked:
            pl.when((slot >= 0) & (slot <= 2 * REACH))(action)
        else:
            action()

    def send(self, number, low, high):
        for n, slot in enumerate(self.slots):
            copy = pltpu.make_async_copy(
                self.tiles.at[n, low:high],
                self.out_ref.at[slot, low:high],
                self.sems.at[number * len(self.slots) + n],
            )
            self.sent.append((slot, copy))
            self.act(slot, copy.start)

    def wait(self):
        for slot, copy in self.sent:
            self.act(slot, copy.wait)


def slot_of(plane, swap_x, swap_core):
    place = lax.rem(lax.axis_index("chan"), QUAD)
    step_x = 2 - 4 * lax.div(place, 2)
    step_core = 1 - 2 * lax.rem(place, 2)
    return REACH + QUAD * plane + swap_x * step_x + swap_core * step_core


def near_kernel(rows_ref, scale_ref, own_ref, sibling_ref, out_ref, window, tiles, sems):
    width = own_ref.shape[1]
    slots = []
    for core, ref in enumerate((own_ref, sibling_ref)):
        for x in range(2):
            n = len(slots)
            window[n * width : (n + 1) * width] = ref[x]
            slots.append(slot_of(0, x, core))
    scale = [scale_ref[pl.ds(slot, 1), :] for slot in slots]
    sender = Sender(tiles, slots, out_ref, sems, False)
    multiply(rows_ref, window, scale, tiles, sender.send)
    sender.wait()


def far_slots(core):
    chan = lax.axis_index("chan")
    place = lax.rem(chan, QUAD)
    ahead = 1 - 2 * lax.rem(lax.div(chan, QUAD), 2)
    slots, stands = [], []
    for plane in (ahead, -ahead):
        for x in range(2):
            slot = slot_of(plane, x, core)
            low = (place == 0) & (plane == 1)
            high = (place == QUAD - 1) & (plane == -1)
            if core == 0 and x == 1:
                stands.append((len(slots), low | high))
                slot = jnp.where(low, 0, jnp.where(high, 2 * REACH, slot))
            slots.append(slot)
    return slots, stands


def own_kernel(rows_ref, scale_ref, first_ref, second_ref, corner_ref, tiles_ref, window):
    width = first_ref.shape[1]
    slots, stands = far_slots(0)
    for n in range(QUAD):
        window[n * width : (n + 1) * width] = (first_ref, second_ref)[n // 2][n % 2]
    for n, stand in stands:

        @pl.when(stand)
        def _():
            window[n * width : (n + 1) * width] = corner_ref[...]

    scale = [scale_ref[pl.ds(jnp.clip(slot, 0, 2 * REACH), 1), :] for slot in slots]
    multiply(rows_ref, window, scale, tiles_ref, lambda *stretch: None)


def sibling_kernel(rows_ref, scale_ref, first_ref, second_ref, own_tiles_ref, near_ref, out_ref, window, tiles, sems,
                   own_sems):
    del near_ref
    width = first_ref.shape[1]
    own_sender = Sender(own_tiles_ref, far_slots(0)[0], out_ref, own_sems, True)
    own_sender.send(0, 0, own_tiles_ref.shape[1])
    slots, _ = far_slots(1)
    for n in range(QUAD):
        window[n * width : (n + 1) * width] = (first_ref, second_ref)[n // 2][n % 2]
    scale = [scale_ref[pl.ds(jnp.clip(slot, 0, 2 * REACH), 1), :] for slot in slots]
    sender = Sender(tiles, slots, out_ref, sems, True)
    multiply(rows_ref, window, scale, tiles, sender.send)
    own_sender.wait()
    sender.wait()


def lag_rows(quad, samples, half):
    depth = quad.shape[2]
    vmem = pl.BlockSpec(memory_space=pltpu.VMEM)
    return pl.pallas_call(
        functools.partial(turn_rows, samples),
        out_shape=jax.ShapeDtypeStruct((2, LAGS * half // 2, depth), jnp.bfloat16),
        in_specs=[vmem],
        out_specs=vmem,
        scratch_shapes=[
            pltpu.VMEM((half, 128), jnp.float32),
            pltpu.VMEM((2, half // 2, depth), jnp.float32),
            pltpu.VMEM((LAGS, BAND), jnp.float32),
            pltpu.VMEM((LAGS, BAND), jnp.float32),
        ],
        compiler_params=pltpu.CompilerParams(vmem_limit_bytes=KERNEL_VMEM),
        cost_estimate=pl.CostEstimate(flops=5*10**9, bytes_accessed=2**20, transcendentals=0),
    )(quad)


def correlate(kernel, operands, out=None, tiles_only=False):
    rows, scale, blobs = operands[:3]
    width, depth = blobs.shape[-2:]
    lines = rows.shape[1]
    vmem = pl.BlockSpec(memory_space=pltpu.VMEM)
    anywhere = pl.BlockSpec(memory_space=pl.ANY)
    extra = [] if out is None else [out]
    scratch = [pltpu.VMEM((QUAD * width, depth), jnp.bfloat16)]
    if not tiles_only:
        scratch += [pltpu.VMEM((QUAD, lines, 2 * width), jnp.float32), pltpu.SemaphoreType.DMA((3 * QUAD,))]
    if extra:
        scratch += [pltpu.SemaphoreType.DMA((QUAD,))]
    return pl.pallas_call(
        kernel,
        out_shape=jax.ShapeDtypeStruct((QUAD if tiles_only else scale.shape[0], lines, 2 * width), jnp.float32),
        in_specs=[vmem] * len(operands) + [anywhere] * len(extra),
        out_specs=vmem if tiles_only else anywhere,
        scratch_shapes=scratch,
        input_output_aliases={len(operands): 0} if extra else {},
        compiler_params=pltpu.CompilerParams(vmem_limit_bytes=KERNEL_VMEM),
        cost_estimate=pl.CostEstimate(
            flops=4 * lines * depth * QUAD * width, bytes_accessed=8 * QUAD * lines * width, transcendentals=0
        ),
    )(*operands, *extra)


def local(traces, partners):
    slots = partners.shape[1]
    segments = lax.axis_size("seg")
    blocks = lax.axis_size("chan")
    channels = traces.shape[1]
    half = channels // segments
    assert segments == 2 and blocks % QUAD == 0 and slots == 2 * REACH + 1
    plane_one = [(c, c ^ QUAD) for c in range(blocks)]
    plane_two = [(c, ((c + QUAD) ^ QUAD) - QUAD) for c in range(QUAD, blocks - QUAD)]
    sibling = [(c, c ^ 1) for c in range(blocks)]
    corners = [(c, c + REACH) for c in range(QUAD - 1, blocks - REACH, QUAD)]
    corners += [(c, c - REACH) for c in range(2 * QUAD, blocks, QUAD)]
    norm_scale = (segments * BAND) ** (-0.5)
    scale = jnp.where(partners[0] >= 0, norm_scale, 0.0).astype(jnp.float32)
    scale = jnp.broadcast_to(scale[:, None], (slots, 2 * channels))
    white = spectra(traces[0])
    corner = lax.ppermute(white, "chan", corners)
    other = lax.ppermute(white, "seg", [(0, 1), (1, 0)])
    across = lax.ppermute(white, "chan", [(c, c ^ 2) for c in range(blocks)])
    diagonal = [(s * blocks + c, (1 - s) * blocks + (c ^ 2)) for s in range(segments) for c in range(blocks)]
    diagonal = lax.ppermute(white, ("seg", "chan"), diagonal)
    pair = jnp.concatenate([white, other], axis=1)
    quad = jnp.stack([pair, jnp.concatenate([across, diagonal], axis=1)])
    quad, scale = lax.optimization_barrier((quad, scale))
    first = lax.ppermute(quad, "chan", plane_one)
    second = lax.ppermute(quad, "chan", plane_two)
    corner_other = lax.ppermute(corner, "seg", [(0, 1), (1, 0)])
    scale, corner, corner_other = lax.optimization_barrier((scale, corner, corner_other))
    near = quad
    corner = jnp.concatenate([corner, corner_other], axis=1)
    beside = lax.ppermute(near, "chan", sibling)
    rows = lag_rows(near, traces.shape[2], half)
    out = correlate(near_kernel, [rows, scale, near, beside])
    first, second, out = lax.optimization_barrier((first, second, out))
    sib_first = lax.ppermute(first, "chan", sibling)
    sib_second = lax.ppermute(second, "chan", sibling)
    tiles = correlate(own_kernel, [rows, scale, first, second, corner], tiles_only=True)
    out = correlate(sibling_kernel, [rows, scale, sib_first, sib_second, tiles], out)
    return out.reshape(1, slots, LAGS, half * channels)


def solution(mesh):
    placed = (P("seg", "chan", None), P("chan", None))
    return jax.shard_map(
        local, mesh=mesh, in_specs=placed, out_specs=P("chan", None, None, "seg"), check_vma=False
    )
```

```python
import functools
import math

import jax
import jax.numpy as jnp
import numpy as np
from jax import lax
from jax.experimental import pallas as pl
from jax.experimental.pallas import tpu as pltpu
from jax.sharding import PartitionSpec as P

BAND = 256
BAND_LO = 16
LAG = 32
LAGS = 2 * LAG + 1
REACH = 5
QUAD = 4
SPECTRUM_VMEM = 55040 * 2**10
KERNEL_VMEM = 24 * 2**20

water_level = 0.5
epsilon = 1e-06


def split_table(samples, step):
    bins = np.arange(BAND) + BAND_LO
    angle = (np.arange(step)[:, None] * bins[None, :] % samples) * (2.0 * math.pi / samples)
    table = np.concatenate([np.cos(angle), -np.sin(angle)], axis=1).astype(np.float32)
    high = table.astype(jnp.bfloat16)
    low = (table - high.astype(np.float32)).astype(jnp.bfloat16)
    return np.stack([high, low])


def spectrum_kernel(step, traces_hbm, table_hbm, white_ref, traces, table, sems):
    channels = white_ref.shape[0]
    stretches = traces.shape[0] // channels
    group = 4
    table_copy = pltpu.make_async_copy(table_hbm, table, sems.at[stretches])
    table_copy.start()
    copies = [
        pltpu.make_async_copy(
            traces_hbm.at[:, pl.ds(n * step, step)], traces.at[pl.ds(n * channels, channels)], sems.at[n]
        )
        for n in range(stretches)
    ]
    for copy in copies:
        copy.start()
    number = lax.broadcasted_iota(jnp.int32, (stretches, BAND), 0)
    bins = lax.broadcasted_iota(jnp.int32, (stretches, BAND), 1) + BAND_LO
    turn = lax.rem(number * bins, stretches).astype(jnp.float32) * (2.0 * math.pi / stretches)
    turn_cos, turn_sin = jnp.cos(turn), jnp.sin(turn)
    table_copy.wait()
    real = imag = None
    for start in range(0, stretches, group):
        for copy in copies[start : start + group]:
            copy.wait()
        part = traces[start * channels : (start + group) * channels]
        y = jnp.dot(part, table[0], preferred_element_type=jnp.float32)
        y = y + jnp.dot(part, table[1], preferred_element_type=jnp.float32)
        for n in range(group):
            y_real = y[n * channels : (n + 1) * channels, :BAND]
            y_imag = y[n * channels : (n + 1) * channels, BAND:]
            if start + n == 0:
                real, imag = y_real, y_imag
                continue
            cosine, sine = turn_cos[start + n : start + n + 1], turn_sin[start + n : start + n + 1]
            real = real + (y_real * cosine + y_imag * sine)
            imag = imag + (y_imag * cosine - y_real * sine)
    power = real * real + imag * imag
    level = jnp.mean(power, axis=1, keepdims=True)
    denom = jnp.sqrt(power + water_level * level + epsilon)
    white_ref[:, :BAND] = (real / denom).astype(jnp.bfloat16)
    white_ref[:, BAND:] = (imag / denom).astype(jnp.bfloat16)


def spectra(traces):
    channels, samples = traces.shape
    step = 256
    table = split_table(samples, step)
    hbm = pl.BlockSpec(memory_space=pltpu.HBM)
    return pl.pallas_call(
        functools.partial(spectrum_kernel, step),
        out_shape=jax.ShapeDtypeStruct((channels, 2 * BAND), jnp.bfloat16),
        in_specs=[hbm] * 2,
        out_specs=pl.BlockSpec(memory_space=pltpu.VMEM),
        scratch_shapes=[
            pltpu.VMEM((samples // step * channels, step), traces.dtype),
            pltpu.VMEM(table.shape, jnp.bfloat16),
            pltpu.SemaphoreType.DMA((samples // step + 1,)),
        ],
        compiler_params=pltpu.CompilerParams(vmem_limit_bytes=SPECTRUM_VMEM),
    )(traces, jnp.asarray(table))


def quad_kernel(white_ref, other_ref, across_ref, diagonal_ref, quad_ref):
    half = white_ref.shape[1]
    quad_ref[0, :, :half] = white_ref[...]
    quad_ref[0, :, half:] = other_ref[...]
    quad_ref[1, :, :half] = across_ref[...]
    quad_ref[1, :, half:] = diagonal_ref[...]


def assemble(*quarters):
    channels, depth = quarters[0].shape
    vmem = pl.BlockSpec(memory_space=pltpu.VMEM)
    return pl.pallas_call(
        quad_kernel,
        out_shape=jax.ShapeDtypeStruct((2, channels, 2 * depth), quarters[0].dtype),
        in_specs=[vmem] * 4,
        out_specs=vmem,
        compiler_params=pltpu.CompilerParams(vmem_limit_bytes=2 * 2**20),
        cost_estimate=pl.CostEstimate(flops=10**9, bytes_accessed=2**19, transcendentals=0),
    )(*quarters)


def rows_kernel(samples, norm_scale, pair_ref, partners_ref, rows_ref, scale_ref, stage, own, lag_cos, lag_sin):
    slots = scale_ref.shape[0]
    slot = lax.broadcasted_iota(jnp.int32, (slots, slots), 0) == lax.broadcasted_iota(jnp.int32, (slots, slots), 1)
    factor = jnp.where(slot & (jnp.broadcast_to(partners_ref[...], (slots, slots)) >= 0), norm_scale, 0.0)
    scale_ref[...] = jnp.broadcast_to(jnp.sum(factor, axis=1, keepdims=True), scale_ref.shape)
    lag = lax.broadcasted_iota(jnp.int32, lag_cos.shape, 0)
    bins = lax.broadcasted_iota(jnp.int32, lag_cos.shape, 1) + BAND_LO
    angle = lax.rem((lag + (samples - LAG)) * bins, samples).astype(jnp.float32) * (2.0 * math.pi / samples)
    lag_cos[...] = jnp.cos(angle)
    lag_sin[...] = jnp.sin(angle)
    pairs = own.shape[1]
    first = pl.multiple_of(lax.axis_index("seg") * 2 * pairs, 2 * pairs)
    mine = pair_ref[0, pl.ds(first, 2 * pairs), :].astype(jnp.float32)
    for left in range(0, mine.shape[1], 128):
        stage[...] = mine[:, left : left + 128]
        for member in range(2):
            own[member, :, left : left + 128] = stage[pl.ds(member, pairs, stride=2), :]

    def turn(lag, carry):
        cosine, sine = lag_cos[pl.ds(lag, 1), :], lag_sin[pl.ds(lag, 1), :]
        at = pl.ds(pl.multiple_of(lag * pairs, pairs), pairs)
        for member in range(2):
            for left in range(0, own.shape[2], 2 * BAND):
                middle, right = left + BAND, left + 2 * BAND
                real, imag = own[member, :, left:middle], own[member, :, middle:right]
                rows_ref[member, at, left:middle] = (real * cosine - imag * sine).astype(jnp.bfloat16)
                rows_ref[member, at, middle:right] = (real * sine + imag * cosine).astype(jnp.bfloat16)
        return carry

    lax.fori_loop(0, LAGS, turn, 0, unroll=5)


def multiply(rows_ref, window, scale, tiles, done):
    members = len(scale)
    width = window.shape[0] // members
    lines = rows_ref.shape[1]
    bounds = [lines * cut // 13 // 16 * 16 for cut in (0, 6, 10)] + [lines]
    for number, (low, high) in enumerate(zip(bounds[:-1], bounds[1:])):
        even, odd = [
            lax.dot_general(
                rows_ref[m, low:high], window[...], (((1,), (1,)), ((), ())), preferred_element_type=jnp.float32
            )
            for m in range(2)
        ]
        lane = lax.broadcasted_iota(jnp.int32, (high - low, 2 * width), 1)
        for n in range(0, members, 2):
            a, b = even[:, n * width : (n + 2) * width], odd[:, n * width : (n + 2) * width]
            tiles[n, low:high] = jnp.where(lane < width, a, pltpu.roll(b, width, 1)) * scale[n]
            tiles[n + 1, low:high] = jnp.where(lane < width, pltpu.roll(a, width, 1), b) * scale[n + 1]
        done(number, low, high)


class Sender:
    def __init__(self, tiles, slots, out_ref, sems, checked):
        self.tiles, self.slots, self.out_ref, self.sems, self.checked = tiles, slots, out_ref, sems, checked
        self.sent = []

    def act(self, slot, action):
        if self.checked:
            pl.when((slot >= 0) & (slot <= 2 * REACH))(action)
        else:
            action()

    def send(self, number, low, high):
        for n, slot in enumerate(self.slots):
            copy = pltpu.make_async_copy(
                self.tiles.at[n, low:high],
                self.out_ref.at[slot, low:high],
                self.sems.at[number * len(self.slots) + n],
            )
            self.sent.append((slot, copy))
            self.act(slot, copy.start)

    def wait(self):
        for slot, copy in self.sent:
            self.act(slot, copy.wait)


def slot_of(plane, swap_x, swap_core):
    place = lax.rem(lax.axis_index("chan"), QUAD)
    step_x = 2 - 4 * lax.div(place, 2)
    step_core = 1 - 2 * lax.rem(place, 2)
    return REACH + QUAD * plane + swap_x * step_x + swap_core * step_core


def near_kernel(rows_ref, scale_ref, own_ref, sibling_ref, out_ref, window, tiles, sems):
    width = own_ref.shape[1]
    slots = []
    for core, ref in enumerate((own_ref, sibling_ref)):
        for x in range(2):
            n = len(slots)
            window[n * width : (n + 1) * width] = ref[x]
            slots.append(slot_of(0, x, core))
    scale = [scale_ref[pl.ds(slot, 1), :] for slot in slots]
    sender = Sender(tiles, slots, out_ref, sems, False)
    multiply(rows_ref, window, scale, tiles, sender.send)
    sender.wait()


def far_slots(core):
    chan = lax.axis_index("chan")
    place = lax.rem(chan, QUAD)
    ahead = 1 - 2 * lax.rem(lax.div(chan, QUAD), 2)
    slots, stands = [], []
    for plane in (ahead, -ahead):
        for x in range(2):
            slot = slot_of(plane, x, core)
            low = (place == 0) & (plane == 1)
            high = (place == QUAD - 1) & (plane == -1)
            if core == 0 and x == 1:
                stands.append((len(slots), low | high))
                slot = jnp.where(low, 0, jnp.where(high, 2 * REACH, slot))
            slots.append(slot)
    return slots, stands


def own_kernel(rows_ref, scale_ref, first_ref, second_ref, corner_ref, tiles_ref, window):
    width = first_ref.shape[1]
    slots, stands = far_slots(0)
    for n in range(QUAD):
        window[n * width : (n + 1) * width] = (first_ref, second_ref)[n // 2][n % 2]
    for n, stand in stands:

        @pl.when(stand)
        def _():
            window[n * width : (n + 1) * width] = corner_ref[...]

    scale = [scale_ref[pl.ds(jnp.clip(slot, 0, 2 * REACH), 1), :] for slot in slots]
    multiply(rows_ref, window, scale, tiles_ref, lambda *stretch: None)


def sibling_kernel(rows_ref, scale_ref, first_ref, second_ref, own_tiles_ref, near_ref, out_ref, window, tiles, sems,
                   own_sems):
    del near_ref
    width = first_ref.shape[1]
    own_sender = Sender(own_tiles_ref, far_slots(0)[0], out_ref, own_sems, True)
    own_sender.send(0, 0, own_tiles_ref.shape[1])
    slots, _ = far_slots(1)
    for n in range(QUAD):
        window[n * width : (n + 1) * width] = (first_ref, second_ref)[n // 2][n % 2]
    scale = [scale_ref[pl.ds(jnp.clip(slot, 0, 2 * REACH), 1), :] for slot in slots]
    sender = Sender(tiles, slots, out_ref, sems, True)
    multiply(rows_ref, window, scale, tiles, sender.send)
    own_sender.wait()
    sender.wait()


def lag_rows(quad, partners, samples, half, norm_scale):
    width, depth = quad.shape[1:]
    vmem = pl.BlockSpec(memory_space=pltpu.VMEM)
    return pl.pallas_call(
        functools.partial(rows_kernel, samples, norm_scale),
        out_shape=[
            jax.ShapeDtypeStruct((2, LAGS * half // 2, depth), jnp.bfloat16),
            jax.ShapeDtypeStruct((partners.shape[1], 2 * width), jnp.float32),
        ],
        in_specs=[vmem, vmem],
        out_specs=[vmem, vmem],
        scratch_shapes=[
            pltpu.VMEM((half, 128), jnp.float32),
            pltpu.VMEM((2, half // 2, depth), jnp.float32),
            pltpu.VMEM((LAGS, BAND), jnp.float32),
            pltpu.VMEM((LAGS, BAND), jnp.float32),
        ],
        compiler_params=pltpu.CompilerParams(vmem_limit_bytes=KERNEL_VMEM),
        cost_estimate=pl.CostEstimate(flops=5 * 10**9, bytes_accessed=2**20, transcendentals=0),
    )(quad, partners)


def correlate(kernel, operands, out=None, tiles_only=False):
    rows, scale, blobs = operands[:3]
    width, depth = blobs.shape[-2:]
    lines = rows.shape[1]
    vmem = pl.BlockSpec(memory_space=pltpu.VMEM)
    anywhere = pl.BlockSpec(memory_space=pl.ANY)
    extra = [] if out is None else [out]
    scratch = [pltpu.VMEM((QUAD * width, depth), jnp.bfloat16)]
    if not tiles_only:
        scratch += [pltpu.VMEM((QUAD, lines, 2 * width), jnp.float32), pltpu.SemaphoreType.DMA((3 * QUAD,))]
    if extra:
        scratch += [pltpu.SemaphoreType.DMA((QUAD,))]
    return pl.pallas_call(
        kernel,
        out_shape=jax.ShapeDtypeStruct((QUAD if tiles_only else scale.shape[0], lines, 2 * width), jnp.float32),
        in_specs=[vmem] * len(operands) + [anywhere] * len(extra),
        out_specs=vmem if tiles_only else anywhere,
        scratch_shapes=scratch,
        input_output_aliases={len(operands): 0} if extra else {},
        compiler_params=pltpu.CompilerParams(vmem_limit_bytes=KERNEL_VMEM),
        cost_estimate=pl.CostEstimate(
            flops=4 * lines * depth * QUAD * width, bytes_accessed=8 * QUAD * lines * width, transcendentals=0
        ),
    )(*operands, *extra)


def local(traces, partners):
    slots = partners.shape[1]
    segments = lax.axis_size("seg")
    blocks = lax.axis_size("chan")
    channels = traces.shape[1]
    half = channels // segments
    assert segments == 2 and blocks % QUAD == 0 and slots == 2 * REACH + 1
    plane_one = [(c, c ^ QUAD) for c in range(blocks)]
    plane_two = [(c, ((c + QUAD) ^ QUAD) - QUAD) for c in range(QUAD, blocks - QUAD)]
    sibling = [(c, c ^ 1) for c in range(blocks)]
    corners = [(c, c + REACH) for c in range(QUAD - 1, blocks - REACH, QUAD)]
    corners += [(c, c - REACH) for c in range(2 * QUAD, blocks, QUAD)]
    norm_scale = (segments * BAND) ** (-0.5)
    white = spectra(traces[0])
    corner = lax.ppermute(white, "chan", corners)
    other = lax.ppermute(white, "seg", [(0, 1), (1, 0)])
    across = lax.ppermute(white, "chan", [(c, c ^ 2) for c in range(blocks)])
    diagonal = [(s * blocks + c, (1 - s) * blocks + (c ^ 2)) for s in range(segments) for c in range(blocks)]
    diagonal = lax.ppermute(white, ("seg", "chan"), diagonal)
    quad = assemble(white, other, across, diagonal)
    first = lax.ppermute(quad, "chan", plane_one)
    second = lax.ppermute(quad, "chan", plane_two)
    near, corner = lax.optimization_barrier((quad, corner))
    corner_other = lax.ppermute(corner, "seg", [(0, 1), (1, 0)])
    beside = lax.ppermute(quad, "chan", sibling)
    rows, scale = lag_rows(near, partners, traces.shape[2], half, norm_scale)
    out = correlate(near_kernel, [rows, scale, quad, beside])
    corner = jnp.concatenate([corner, corner_other], axis=1)
    first, second, out = lax.optimization_barrier((first, second, out))
    sib_first = lax.ppermute(first, "chan", sibling)
    sib_second = lax.ppermute(second, "chan", sibling)
    tiles = correlate(own_kernel, [rows, scale, first, second, corner], tiles_only=True)
    out = correlate(sibling_kernel, [rows, scale, sib_first, sib_second, tiles], out)
    return out.reshape(1, slots, LAGS, half * channels)


def solution(mesh):
    placed = (P("seg", "chan", None), P("chan", None))
    return jax.shard_map(
        local, mesh=mesh, in_specs=placed, out_specs=P("chan", None, None, "seg"), check_vma=False
    )
```

```python
import functools
import math

import jax
import jax.numpy as jnp
import numpy as np
from jax import lax
from jax.experimental import pallas as pl
from jax.experimental.pallas import tpu as pltpu
from jax.sharding import PartitionSpec as P

BAND = 256
BAND_LO = 16
LAG = 32
LAGS = 2 * LAG + 1
REACH = 5
QUAD = 4
SPECTRUM_VMEM = 55040 * 2**10
KERNEL_VMEM = 24 * 2**20

water_level = 0.5
epsilon = 1e-06


def split_table(samples, step):
    bins = np.arange(BAND) + BAND_LO
    angle = (np.arange(step)[:, None] * bins[None, :] % samples) * (2.0 * math.pi / samples)
    table = np.concatenate([np.cos(angle), -np.sin(angle)], axis=1).astype(np.float32)
    high = table.astype(jnp.bfloat16)
    low = (table - high.astype(np.float32)).astype(jnp.bfloat16)
    return np.stack([high, low])


def spectrum_kernel(step, traces_hbm, table_hbm, white_ref, traces, table, sems):
    channels = white_ref.shape[0]
    stretches = traces.shape[0] // channels
    group = 4
    table_copy = pltpu.make_async_copy(table_hbm, table, sems.at[stretches])
    table_copy.start()
    copies = [
        pltpu.make_async_copy(
            traces_hbm.at[:, pl.ds(n * step, step)], traces.at[pl.ds(n * channels, channels)], sems.at[n]
        )
        for n in range(stretches)
    ]
    for copy in copies:
        copy.start()
    number = lax.broadcasted_iota(jnp.int32, (stretches, BAND), 0)
    bins = lax.broadcasted_iota(jnp.int32, (stretches, BAND), 1) + BAND_LO
    turn = lax.rem(number * bins, stretches).astype(jnp.float32) * (2.0 * math.pi / stretches)
    turn_cos, turn_sin = jnp.cos(turn), jnp.sin(turn)
    table_copy.wait()
    real = imag = None
    for start in range(0, stretches, group):
        for copy in copies[start : start + group]:
            copy.wait()
        part = traces[start * channels : (start + group) * channels]
        y = jnp.dot(part, table[0], preferred_element_type=jnp.float32)
        y = y + jnp.dot(part, table[1], preferred_element_type=jnp.float32)
        for n in range(group):
            y_real = y[n * channels : (n + 1) * channels, :BAND]
            y_imag = y[n * channels : (n + 1) * channels, BAND:]
            if start + n == 0:
                real, imag = y_real, y_imag
                continue
            cosine, sine = turn_cos[start + n : start + n + 1], turn_sin[start + n : start + n + 1]
            real = real + (y_real * cosine + y_imag * sine)
            imag = imag + (y_imag * cosine - y_real * sine)
    power = real * real + imag * imag
    level = jnp.mean(power, axis=1, keepdims=True)
    denom = jnp.sqrt(power + water_level * level + epsilon)
    white_ref[:, :BAND] = (real / denom).astype(jnp.bfloat16)
    white_ref[:, BAND:] = (imag / denom).astype(jnp.bfloat16)


def spectra(traces):
    channels, samples = traces.shape
    step = 256
    table = split_table(samples, step)
    hbm = pl.BlockSpec(memory_space=pltpu.HBM)
    return pl.pallas_call(
        functools.partial(spectrum_kernel, step),
        out_shape=jax.ShapeDtypeStruct((channels, 2 * BAND), jnp.bfloat16),
        in_specs=[hbm] * 2,
        out_specs=pl.BlockSpec(memory_space=pltpu.VMEM),
        scratch_shapes=[
            pltpu.VMEM((samples // step * channels, step), traces.dtype),
            pltpu.VMEM(table.shape, jnp.bfloat16),
            pltpu.SemaphoreType.DMA((samples // step + 1,)),
        ],
        compiler_params=pltpu.CompilerParams(vmem_limit_bytes=SPECTRUM_VMEM),
    )(traces, jnp.asarray(table))


def quad_kernel(white_ref, other_ref, across_ref, diagonal_ref, quad_ref):
    half = white_ref.shape[1]
    quad_ref[0, :, :half] = white_ref[...]
    quad_ref[0, :, half:] = other_ref[...]
    quad_ref[1, :, :half] = across_ref[...]
    quad_ref[1, :, half:] = diagonal_ref[...]


def assemble(*quarters):
    channels, depth = quarters[0].shape
    vmem = pl.BlockSpec(memory_space=pltpu.VMEM)
    return pl.pallas_call(
        quad_kernel,
        out_shape=jax.ShapeDtypeStruct((2, channels, 2 * depth), quarters[0].dtype),
        in_specs=[vmem] * 4,
        out_specs=vmem,
        compiler_params=pltpu.CompilerParams(vmem_limit_bytes=2 * 2**20),
        cost_estimate=pl.CostEstimate(flops=10**9, bytes_accessed=2**19, transcendentals=0),
    )(*quarters)


def rows_kernel(samples, norm_scale, pair_ref, partners_ref, rows_ref, scale_ref, stage, own, lag_cos, lag_sin):
    slots = scale_ref.shape[0]
    slot = lax.broadcasted_iota(jnp.int32, (slots, slots), 0) == lax.broadcasted_iota(jnp.int32, (slots, slots), 1)
    factor = jnp.where(slot & (jnp.broadcast_to(partners_ref[...], (slots, slots)) >= 0), norm_scale, 0.0)
    scale_ref[...] = jnp.broadcast_to(jnp.sum(factor, axis=1, keepdims=True), scale_ref.shape)
    lag = lax.broadcasted_iota(jnp.int32, lag_cos.shape, 0)
    bins = lax.broadcasted_iota(jnp.int32, lag_cos.shape, 1) + BAND_LO
    angle = lax.rem((lag + (samples - LAG)) * bins, samples).astype(jnp.float32) * (2.0 * math.pi / samples)
    lag_cos[...] = jnp.cos(angle)
    lag_sin[...] = jnp.sin(angle)
    pairs = own.shape[1]
    first = pl.multiple_of(lax.axis_index("seg") * 2 * pairs, 2 * pairs)
    mine = pair_ref[0, pl.ds(first, 2 * pairs), :].astype(jnp.float32)
    for left in range(0, mine.shape[1], 128):
        stage[...] = mine[:, left : left + 128]
        for member in range(2):
            own[member, :, left : left + 128] = stage[pl.ds(member, pairs, stride=2), :]

    def turn(lag, carry):
        cosine, sine = lag_cos[pl.ds(lag, 1), :], lag_sin[pl.ds(lag, 1), :]
        at = pl.ds(pl.multiple_of(lag * pairs, pairs), pairs)
        for member in range(2):
            for left in range(0, own.shape[2], 2 * BAND):
                middle, right = left + BAND, left + 2 * BAND
                real, imag = own[member, :, left:middle], own[member, :, middle:right]
                rows_ref[member, at, left:middle] = (real * cosine - imag * sine).astype(jnp.bfloat16)
                rows_ref[member, at, middle:right] = (real * sine + imag * cosine).astype(jnp.bfloat16)
        return carry

    lax.fori_loop(0, LAGS, turn, 0, unroll=5)


def multiply(rows_ref, window, scale, tiles, done):
    members = len(scale)
    width = window.shape[0] // members
    lines = rows_ref.shape[1]
    bounds = [lines * cut // 13 // 16 * 16 for cut in (0, 6, 10)] + [lines]
    for number, (low, high) in enumerate(zip(bounds[:-1], bounds[1:])):
        even, odd = [
            lax.dot_general(
                rows_ref[m, low:high], window[...], (((1,), (1,)), ((), ())), preferred_element_type=jnp.float32
            )
            for m in range(2)
        ]
        lane = lax.broadcasted_iota(jnp.int32, (high - low, 2 * width), 1)
        for n in range(0, members, 2):
            a, b = even[:, n * width : (n + 2) * width], odd[:, n * width : (n + 2) * width]
            tiles[n, low:high] = jnp.where(lane < width, a, pltpu.roll(b, width, 1)) * scale[n]
            tiles[n + 1, low:high] = jnp.where(lane < width, pltpu.roll(a, width, 1), b) * scale[n + 1]
        done(number, low, high)


class Sender:
    def __init__(self, tiles, slots, out_ref, sems, checked):
        self.tiles, self.slots, self.out_ref, self.sems, self.checked = tiles, slots, out_ref, sems, checked
        self.sent = []

    def act(self, slot, action):
        if self.checked:
            pl.when((slot >= 0) & (slot <= 2 * REACH))(action)
        else:
            action()

    def send(self, number, low, high):
        for n, slot in enumerate(self.slots):
            copy = pltpu.make_async_copy(
                self.tiles.at[n, low:high],
                self.out_ref.at[slot, low:high],
                self.sems.at[number * len(self.slots) + n],
            )
            self.sent.append((slot, copy))
            self.act(slot, copy.start)

    def wait(self):
        for slot, copy in self.sent:
            self.act(slot, copy.wait)


def slot_of(plane, swap_x, swap_core):
    place = lax.rem(lax.axis_index("chan"), QUAD)
    step_x = 2 - 4 * lax.div(place, 2)
    step_core = 1 - 2 * lax.rem(place, 2)
    return REACH + QUAD * plane + swap_x * step_x + swap_core * step_core


def near_kernel(rows_ref, scale_ref, own_ref, sibling_ref, out_ref, window, tiles, sems):
    width = own_ref.shape[1]
    slots = []
    for core, ref in enumerate((own_ref, sibling_ref)):
        for x in range(2):
            n = len(slots)
            window[n * width : (n + 1) * width] = ref[x]
            slots.append(slot_of(0, x, core))
    scale = [scale_ref[pl.ds(slot, 1), :] for slot in slots]
    sender = Sender(tiles, slots, out_ref, sems, False)
    multiply(rows_ref, window, scale, tiles, sender.send)
    sender.wait()


def far_slots(core):
    chan = lax.axis_index("chan")
    place = lax.rem(chan, QUAD)
    ahead = 2 * lax.rem(lax.div(chan, QUAD), 2) - 1
    slots, stands = [], []
    for plane in (ahead, -ahead):
        for x in range(2):
            slot = slot_of(plane, x, core)
            low = (place == 0) & (plane == 1)
            high = (place == QUAD - 1) & (plane == -1)
            if core == 0 and x == 1:
                stands.append((len(slots), low | high))
                slot = jnp.where(low, 0, jnp.where(high, 2 * REACH, slot))
            slots.append(slot)
    return slots, stands


def own_kernel(rows_ref, scale_ref, first_ref, second_ref, corner_ref, tiles_ref, window):
    width = first_ref.shape[1]
    slots, stands = far_slots(0)
    for n in range(QUAD):
        window[n * width : (n + 1) * width] = (first_ref, second_ref)[n // 2][n % 2]
    for n, stand in stands:

        @pl.when(stand)
        def _():
            window[n * width : (n + 1) * width] = corner_ref[...]

    scale = [scale_ref[pl.ds(jnp.clip(slot, 0, 2 * REACH), 1), :] for slot in slots]
    multiply(rows_ref, window, scale, tiles_ref, lambda *stretch: None)


def sibling_kernel(rows_ref, scale_ref, first_ref, second_ref, own_tiles_ref, near_ref, out_ref, window, tiles, sems,
                   own_sems):
    del near_ref
    width = first_ref.shape[1]
    own_sender = Sender(own_tiles_ref, far_slots(0)[0], out_ref, own_sems, True)
    own_sender.send(0, 0, own_tiles_ref.shape[1])
    slots, _ = far_slots(1)
    for n in range(QUAD):
        window[n * width : (n + 1) * width] = (first_ref, second_ref)[n // 2][n % 2]
    scale = [scale_ref[pl.ds(jnp.clip(slot, 0, 2 * REACH), 1), :] for slot in slots]
    sender = Sender(tiles, slots, out_ref, sems, True)
    multiply(rows_ref, window, scale, tiles, sender.send)
    own_sender.wait()
    sender.wait()


def lag_rows(quad, partners, samples, half, norm_scale):
    width, depth = quad.shape[1:]
    vmem = pl.BlockSpec(memory_space=pltpu.VMEM)
    return pl.pallas_call(
        functools.partial(rows_kernel, samples, norm_scale),
        out_shape=[
            jax.ShapeDtypeStruct((2, LAGS * half // 2, depth), jnp.bfloat16),
            jax.ShapeDtypeStruct((partners.shape[1], 2 * width), jnp.float32),
        ],
        in_specs=[vmem, vmem],
        out_specs=[vmem, vmem],
        scratch_shapes=[
            pltpu.VMEM((half, 128), jnp.float32),
            pltpu.VMEM((2, half // 2, depth), jnp.float32),
            pltpu.VMEM((LAGS, BAND), jnp.float32),
            pltpu.VMEM((LAGS, BAND), jnp.float32),
        ],
        compiler_params=pltpu.CompilerParams(vmem_limit_bytes=KERNEL_VMEM),
        cost_estimate=pl.CostEstimate(flops=5 * 10**9, bytes_accessed=2**20, transcendentals=0),
    )(quad, partners)


def correlate(kernel, operands, out=None, tiles_only=False):
    rows, scale, blobs = operands[:3]
    width, depth = blobs.shape[-2:]
    lines = rows.shape[1]
    vmem = pl.BlockSpec(memory_space=pltpu.VMEM)
    anywhere = pl.BlockSpec(memory_space=pl.ANY)
    extra = [] if out is None else [out]
    scratch = [pltpu.VMEM((QUAD * width, depth), jnp.bfloat16)]
    if not tiles_only:
        scratch += [pltpu.VMEM((QUAD, lines, 2 * width), jnp.float32), pltpu.SemaphoreType.DMA((3 * QUAD,))]
    if extra:
        scratch += [pltpu.SemaphoreType.DMA((QUAD,))]
    return pl.pallas_call(
        kernel,
        out_shape=jax.ShapeDtypeStruct((QUAD if tiles_only else scale.shape[0], lines, 2 * width), jnp.float32),
        in_specs=[vmem] * len(operands) + [anywhere] * len(extra),
        out_specs=vmem if tiles_only else anywhere,
        scratch_shapes=scratch,
        input_output_aliases={len(operands): 0} if extra else {},
        compiler_params=pltpu.CompilerParams(vmem_limit_bytes=KERNEL_VMEM),
        cost_estimate=pl.CostEstimate(
            flops=4 * lines * depth * QUAD * width, bytes_accessed=8 * QUAD * lines * width, transcendentals=0
        ),
    )(*operands, *extra)


def local(traces, partners):
    slots = partners.shape[1]
    segments = lax.axis_size("seg")
    blocks = lax.axis_size("chan")
    channels = traces.shape[1]
    half = channels // segments
    assert segments == 2 and blocks % QUAD == 0 and slots == 2 * REACH + 1
    plane_two = [(c, c ^ QUAD) for c in range(blocks)]
    plane_one = [(c, ((c + QUAD) ^ QUAD) - QUAD) for c in range(QUAD, blocks - QUAD)]
    sibling = [(c, c ^ 1) for c in range(blocks)]
    corners = [(c, c + REACH) for c in range(QUAD - 1, blocks - REACH, QUAD)]
    corners += [(c, c - REACH) for c in range(2 * QUAD, blocks, QUAD)]
    norm_scale = (segments * BAND) ** (-0.5)
    white = spectra(traces[0])
    corner = lax.ppermute(white, "chan", corners)
    other = lax.ppermute(white, "seg", [(0, 1), (1, 0)])
    across = lax.ppermute(white, "chan", [(c, c ^ 2) for c in range(blocks)])
    diagonal = [(s * blocks + c, (1 - s) * blocks + (c ^ 2)) for s in range(segments) for c in range(blocks)]
    diagonal = lax.ppermute(white, ("seg", "chan"), diagonal)
    quad = assemble(white, other, across, diagonal)
    first = lax.ppermute(quad, "chan", plane_one)
    second = lax.ppermute(quad, "chan", plane_two)
    near, corner = lax.optimization_barrier((quad, corner))
    corner_other = lax.ppermute(corner, "seg", [(0, 1), (1, 0)])
    beside = lax.ppermute(near, "chan", sibling)
    rows, scale = lag_rows(near, partners, traces.shape[2], half, norm_scale)
    out = correlate(near_kernel, [rows, scale, quad, beside])
    corner = jnp.concatenate([corner, corner_other], axis=1)
    first, second, out = lax.optimization_barrier((first, second, out))
    sib_first = lax.ppermute(first, "chan", sibling)
    sib_second = lax.ppermute(second, "chan", sibling)
    tiles = correlate(own_kernel, [rows, scale, first, second, corner], tiles_only=True)
    out = correlate(sibling_kernel, [rows, scale, sib_first, sib_second, tiles], out)
    return out.reshape(1, slots, LAGS, half * channels)


def solution(mesh):
    placed = (P("seg", "chan", None), P("chan", None))
    return jax.shard_map(
        local, mesh=mesh, in_specs=placed, out_specs=P("chan", None, None, "seg"), check_vma=False
    )
```

```python
import functools
import math

import jax
import jax.numpy as jnp
import numpy as np
from jax import lax
from jax.experimental import pallas as pl
from jax.experimental.pallas import tpu as pltpu
from jax.sharding import PartitionSpec as P

BAND = 256
BAND_LO = 16
LAG = 32
LAGS = 2 * LAG + 1
REACH = 5
QUAD = 4
SPECTRUM_VMEM = 55040 * 2**10
KERNEL_VMEM = 24 * 2**20

water_level = 0.5
epsilon = 1e-06


def split_table(samples, step):
    bins = np.arange(BAND) + BAND_LO
    angle = (np.arange(step)[:, None] * bins[None, :] % samples) * (2.0 * math.pi / samples)
    table = np.concatenate([np.cos(angle), -np.sin(angle)], axis=1).astype(np.float32)
    high = table.astype(jnp.bfloat16)
    low = (table - high.astype(np.float32)).astype(jnp.bfloat16)
    return np.stack([high, low])


def spectrum_kernel(step, traces_hbm, table_hbm, white_ref, traces, table, sems):
    channels = white_ref.shape[0]
    stretches = traces.shape[0] // channels
    group = stretches
    table_copy = pltpu.make_async_copy(table_hbm, table, sems.at[stretches])
    table_copy.start()
    copies = [
        pltpu.make_async_copy(
            traces_hbm.at[:, pl.ds(n * step, step)], traces.at[pl.ds(n * channels, channels)], sems.at[n]
        )
        for n in range(stretches)
    ]
    for copy in copies:
        copy.start()
    number = lax.broadcasted_iota(jnp.int32, (stretches, BAND), 0)
    bins = lax.broadcasted_iota(jnp.int32, (stretches, BAND), 1) + BAND_LO
    turn = lax.rem(number * bins, stretches).astype(jnp.float32) * (2.0 * math.pi / stretches)
    turn_cos, turn_sin = jnp.cos(turn), jnp.sin(turn)
    table_copy.wait()
    real = imag = None
    for start in range(0, stretches, group):
        for copy in copies[start : start + group]:
            copy.wait()
        part = traces[start * channels : (start + group) * channels]
        y = jnp.dot(part, table[0], preferred_element_type=jnp.float32)
        y = y + jnp.dot(part, table[1], preferred_element_type=jnp.float32)
        for n in range(group):
            y_real = y[n * channels : (n + 1) * channels, :BAND]
            y_imag = y[n * channels : (n + 1) * channels, BAND:]
            if start + n == 0:
                real, imag = y_real, y_imag
                continue
            cosine, sine = turn_cos[start + n : start + n + 1], turn_sin[start + n : start + n + 1]
            real = real + (y_real * cosine + y_imag * sine)
            imag = imag + (y_imag * cosine - y_real * sine)
    power = real * real + imag * imag
    level = jnp.mean(power, axis=1, keepdims=True)
    denom = jnp.sqrt(power + water_level * level + epsilon)
    white_ref[:, :BAND] = (real / denom).astype(jnp.bfloat16)
    white_ref[:, BAND:] = (imag / denom).astype(jnp.bfloat16)


def spectra(traces):
    channels, samples = traces.shape
    step = 256
    table = split_table(samples, step)
    hbm = pl.BlockSpec(memory_space=pltpu.HBM)
    return pl.pallas_call(
        functools.partial(spectrum_kernel, step),
        out_shape=jax.ShapeDtypeStruct((channels, 2 * BAND), jnp.bfloat16),
        in_specs=[hbm] * 2,
        out_specs=pl.BlockSpec(memory_space=pltpu.VMEM),
        scratch_shapes=[
            pltpu.VMEM((samples // step * channels, step), traces.dtype),
            pltpu.VMEM(table.shape, jnp.bfloat16),
            pltpu.SemaphoreType.DMA((samples // step + 1,)),
        ],
        cost_estimate=pl.CostEstimate(flops=10**9, bytes_accessed=2**20, transcendentals=0),
        compiler_params=pltpu.CompilerParams(vmem_limit_bytes=SPECTRUM_VMEM),
    )(traces, jnp.asarray(table))


def quad_kernel(white_ref, other_ref, across_ref, diagonal_ref, quad_ref):
    half = white_ref.shape[1]
    quad_ref[0, :, :half] = white_ref[...]
    quad_ref[0, :, half:] = other_ref[...]
    quad_ref[1, :, :half] = across_ref[...]
    quad_ref[1, :, half:] = diagonal_ref[...]


def assemble(*quarters):
    channels, depth = quarters[0].shape
    vmem = pl.BlockSpec(memory_space=pltpu.VMEM)
    return pl.pallas_call(
        quad_kernel,
        out_shape=jax.ShapeDtypeStruct((2, channels, 2 * depth), quarters[0].dtype),
        in_specs=[vmem] * 4,
        out_specs=vmem,
        compiler_params=pltpu.CompilerParams(vmem_limit_bytes=2 * 2**20),
        cost_estimate=pl.CostEstimate(flops=10**9, bytes_accessed=2**19, transcendentals=0),
    )(*quarters)


def rows_kernel(samples, norm_scale, pair_ref, partners_ref, rows_ref, scale_ref, stage, own, lag_cos, lag_sin):
    slots = scale_ref.shape[0]
    slot = lax.broadcasted_iota(jnp.int32, (slots, slots), 0) == lax.broadcasted_iota(jnp.int32, (slots, slots), 1)
    factor = jnp.where(slot & (jnp.broadcast_to(partners_ref[...], (slots, slots)) >= 0), norm_scale, 0.0)
    scale_ref[...] = jnp.broadcast_to(jnp.sum(factor, axis=1, keepdims=True), scale_ref.shape)
    lag = lax.broadcasted_iota(jnp.int32, lag_cos.shape, 0)
    bins = lax.broadcasted_iota(jnp.int32, lag_cos.shape, 1) + BAND_LO
    angle = lax.rem((lag + (samples - LAG)) * bins, samples).astype(jnp.float32) * (2.0 * math.pi / samples)
    lag_cos[...] = jnp.cos(angle)
    lag_sin[...] = jnp.sin(angle)
    pairs = own.shape[1]
    first = pl.multiple_of(lax.axis_index("seg") * 2 * pairs, 2 * pairs)
    mine = pair_ref[0, pl.ds(first, 2 * pairs), :].astype(jnp.float32)
    for left in range(0, mine.shape[1], 128):
        stage[...] = mine[:, left : left + 128]
        for member in range(2):
            own[member, :, left : left + 128] = stage[pl.ds(member, pairs, stride=2), :]

    def turn(lag, carry):
        cosine, sine = lag_cos[pl.ds(lag, 1), :], lag_sin[pl.ds(lag, 1), :]
        at = pl.ds(pl.multiple_of(lag * pairs, pairs), pairs)
        for member in range(2):
            for left in range(0, own.shape[2], 2 * BAND):
                middle, right = left + BAND, left + 2 * BAND
                real, imag = own[member, :, left:middle], own[member, :, middle:right]
                rows_ref[member, at, left:middle] = (real * cosine - imag * sine).astype(jnp.bfloat16)
                rows_ref[member, at, middle:right] = (real * sine + imag * cosine).astype(jnp.bfloat16)
        return carry

    lax.fori_loop(0, LAGS, turn, 0, unroll=5)


def multiply(rows_ref, window, scale, tiles, done):
    members = len(scale)
    width = window.shape[0] // members
    lines = rows_ref.shape[1]
    bounds = [lines * cut // 13 // 16 * 16 for cut in (0, 6, 10)] + [lines]
    for number, (low, high) in enumerate(zip(bounds[:-1], bounds[1:])):
        even, odd = [
            lax.dot_general(
                rows_ref[m, low:high], window[...], (((1,), (1,)), ((), ())), preferred_element_type=jnp.float32
            )
            for m in range(2)
        ]
        lane = lax.broadcasted_iota(jnp.int32, (high - low, 2 * width), 1)
        for n in range(0, members, 2):
            a, b = even[:, n * width : (n + 2) * width], odd[:, n * width : (n + 2) * width]
            tiles[n, low:high] = jnp.where(lane < width, a, pltpu.roll(b, width, 1)) * scale[n]
            tiles[n + 1, low:high] = jnp.where(lane < width, pltpu.roll(a, width, 1), b) * scale[n + 1]
        done(number, low, high)


class Sender:
    def __init__(self, tiles, slots, out_ref, sems, checked):
        self.tiles, self.slots, self.out_ref, self.sems, self.checked = tiles, slots, out_ref, sems, checked
        self.sent = []

    def act(self, slot, action):
        if self.checked:
            pl.when((slot >= 0) & (slot <= 2 * REACH))(action)
        else:
            action()

    def send(self, number, low, high):
        for n, slot in enumerate(self.slots):
            copy = pltpu.make_async_copy(
                self.tiles.at[n, low:high],
                self.out_ref.at[slot, low:high],
                self.sems.at[number * len(self.slots) + n],
            )
            self.sent.append((slot, copy))
            self.act(slot, copy.start)

    def wait(self):
        for slot, copy in self.sent:
            self.act(slot, copy.wait)


def slot_of(plane, swap_x, swap_core):
    place = lax.rem(lax.axis_index("chan"), QUAD)
    step_x = 2 - 4 * lax.div(place, 2)
    step_core = 1 - 2 * lax.rem(place, 2)
    return REACH + QUAD * plane + swap_x * step_x + swap_core * step_core


def near_kernel(rows_ref, scale_ref, own_ref, sibling_ref, out_ref, window, tiles, sems):
    width = own_ref.shape[1]
    slots = []
    for core, ref in enumerate((own_ref, sibling_ref)):
        for x in range(2):
            n = len(slots)
            window[n * width : (n + 1) * width] = ref[x]
            slots.append(slot_of(0, x, core))
    scale = [scale_ref[pl.ds(slot, 1), :] for slot in slots]
    sender = Sender(tiles, slots, out_ref, sems, False)
    multiply(rows_ref, window, scale, tiles, sender.send)
    sender.wait()


def far_slots(core):
    chan = lax.axis_index("chan")
    place = lax.rem(chan, QUAD)
    ahead = 2 * lax.rem(lax.div(chan, QUAD), 2) - 1
    slots, stands = [], []
    for plane in (ahead, -ahead):
        for x in range(2):
            slot = slot_of(plane, x, core)
            low = (place == 0) & (plane == 1)
            high = (place == QUAD - 1) & (plane == -1)
            if core == 0 and x == 1:
                stands.append((len(slots), low | high))
                slot = jnp.where(low, 0, jnp.where(high, 2 * REACH, slot))
            slots.append(slot)
    return slots, stands


def own_kernel(rows_ref, scale_ref, first_ref, second_ref, corner_ref, tiles_ref, window):
    width = first_ref.shape[1]
    slots, stands = far_slots(0)
    for n in range(QUAD):
        window[n * width : (n + 1) * width] = (first_ref, second_ref)[n // 2][n % 2]
    for n, stand in stands:

        @pl.when(stand)
        def _():
            window[n * width : (n + 1) * width] = corner_ref[...]

    scale = [scale_ref[pl.ds(jnp.clip(slot, 0, 2 * REACH), 1), :] for slot in slots]
    multiply(rows_ref, window, scale, tiles_ref, lambda *stretch: None)


def sibling_kernel(rows_ref, scale_ref, first_ref, second_ref, own_tiles_ref, near_ref, out_ref, window, tiles, sems,
                   own_sems):
    del near_ref
    width = first_ref.shape[1]
    own_sender = Sender(own_tiles_ref, far_slots(0)[0], out_ref, own_sems, True)
    own_sender.send(0, 0, own_tiles_ref.shape[1])
    slots, _ = far_slots(1)
    for n in range(QUAD):
        window[n * width : (n + 1) * width] = (first_ref, second_ref)[n // 2][n % 2]
    scale = [scale_ref[pl.ds(jnp.clip(slot, 0, 2 * REACH), 1), :] for slot in slots]
    sender = Sender(tiles, slots, out_ref, sems, True)
    multiply(rows_ref, window, scale, tiles, sender.send)
    own_sender.wait()
    sender.wait()


def lag_rows(quad, partners, samples, half, norm_scale):
    width, depth = quad.shape[1:]
    vmem = pl.BlockSpec(memory_space=pltpu.VMEM)
    return pl.pallas_call(
        functools.partial(rows_kernel, samples, norm_scale),
        out_shape=[
            jax.ShapeDtypeStruct((2, LAGS * half // 2, depth), jnp.bfloat16),
            jax.ShapeDtypeStruct((partners.shape[1], 2 * width), jnp.float32),
        ],
        in_specs=[vmem, vmem],
        out_specs=[vmem, vmem],
        scratch_shapes=[
            pltpu.VMEM((half, 128), jnp.float32),
            pltpu.VMEM((2, half // 2, depth), jnp.float32),
            pltpu.VMEM((LAGS, BAND), jnp.float32),
            pltpu.VMEM((LAGS, BAND), jnp.float32),
        ],
        compiler_params=pltpu.CompilerParams(vmem_limit_bytes=KERNEL_VMEM),
        cost_estimate=pl.CostEstimate(flops=5 * 10**9, bytes_accessed=2**20, transcendentals=0),
    )(quad, partners)


def correlate(kernel, operands, out=None, tiles_only=False):
    rows, scale, blobs = operands[:3]
    width, depth = blobs.shape[-2:]
    lines = rows.shape[1]
    vmem = pl.BlockSpec(memory_space=pltpu.VMEM)
    anywhere = pl.BlockSpec(memory_space=pl.ANY)
    extra = [] if out is None else [out]
    scratch = [pltpu.VMEM((QUAD * width, depth), jnp.bfloat16)]
    if not tiles_only:
        scratch += [pltpu.VMEM((QUAD, lines, 2 * width), jnp.float32), pltpu.SemaphoreType.DMA((3 * QUAD,))]
    if extra:
        scratch += [pltpu.SemaphoreType.DMA((QUAD,))]
    return pl.pallas_call(
        kernel,
        out_shape=jax.ShapeDtypeStruct((QUAD if tiles_only else scale.shape[0], lines, 2 * width), jnp.float32),
        in_specs=[vmem] * len(operands) + [anywhere] * len(extra),
        out_specs=vmem if tiles_only else anywhere,
        scratch_shapes=scratch,
        input_output_aliases={len(operands): 0} if extra else {},
        compiler_params=pltpu.CompilerParams(vmem_limit_bytes=KERNEL_VMEM),
        cost_estimate=pl.CostEstimate(
            flops=4 * lines * depth * QUAD * width, bytes_accessed=8 * QUAD * lines * width, transcendentals=0
        ),
    )(*operands, *extra)


def local(traces, partners):
    slots = partners.shape[1]
    segments = lax.axis_size("seg")
    blocks = lax.axis_size("chan")
    channels = traces.shape[1]
    half = channels // segments
    assert segments == 2 and blocks % QUAD == 0 and slots == 2 * REACH + 1
    plane_two = [(c, c ^ QUAD) for c in range(blocks)]
    plane_one = [(c, ((c + QUAD) ^ QUAD) - QUAD) for c in range(QUAD, blocks - QUAD)]
    sibling = [(c, c ^ 1) for c in range(blocks)]
    corners = [(c, c + REACH) for c in range(QUAD - 1, blocks - REACH, QUAD)]
    corners += [(c, c - REACH) for c in range(2 * QUAD, blocks, QUAD)]
    norm_scale = (segments * BAND) ** (-0.5)
    white = spectra(traces[0])
    corner = lax.ppermute(white, "chan", corners)
    other = lax.ppermute(white, "seg", [(0, 1), (1, 0)])
    across = lax.ppermute(white, "chan", [(c, c ^ 2) for c in range(blocks)])
    diagonal = [(s * blocks + c, (1 - s) * blocks + (c ^ 2)) for s in range(segments) for c in range(blocks)]
    diagonal = lax.ppermute(white, ("seg", "chan"), diagonal)
    quad = assemble(white, other, across, diagonal)
    first = lax.ppermute(quad, "chan", plane_one)
    second = lax.ppermute(quad, "chan", plane_two)
    near, corner = lax.optimization_barrier((quad, corner))
    corner_other = lax.ppermute(corner, "seg", [(0, 1), (1, 0)])
    beside = lax.ppermute(near, "chan", sibling)
    rows, scale = lag_rows(near, partners, traces.shape[2], half, norm_scale)
    out = correlate(near_kernel, [rows, scale, quad, beside])
    corner = jnp.concatenate([corner, corner_other], axis=1)
    first, second, out = lax.optimization_barrier((first, second, out))
    sib_first = lax.ppermute(first, "chan", sibling)
    sib_second = lax.ppermute(second, "chan", sibling)
    tiles = correlate(own_kernel, [rows, scale, first, second, corner], tiles_only=True)
    out = correlate(sibling_kernel, [rows, scale, sib_first, sib_second, tiles], out)
    return out.reshape(1, slots, LAGS, half * channels)


def solution(mesh):
    placed = (P("seg", "chan", None), P("chan", None))
    return jax.shard_map(
        local, mesh=mesh, in_specs=placed, out_specs=P("chan", None, None, "seg"), check_vma=False
    )
```

```python
import functools
import math

import jax
import jax.numpy as jnp
import numpy as np
from jax import lax
from jax.experimental import pallas as pl
from jax.experimental.pallas import tpu as pltpu
from jax.sharding import PartitionSpec as P

BAND = 256
BAND_LO = 16
LAG = 32
LAGS = 2 * LAG + 1
REACH = 5
QUAD = 4
SPECTRUM_VMEM = 55040 * 2**10
KERNEL_VMEM = 24 * 2**20

water_level = 0.5
epsilon = 1e-06


def split_table(samples, step):
    bins = np.arange(BAND) + BAND_LO
    angle = (np.arange(step)[:, None] * bins[None, :] % samples) * (2.0 * math.pi / samples)
    table = np.concatenate([np.cos(angle), -np.sin(angle)], axis=1).astype(np.float32)
    high = table.astype(jnp.bfloat16)
    low = (table - high.astype(np.float32)).astype(jnp.bfloat16)
    return np.stack([high, low])


def spectrum_kernel(step, traces_hbm, table_hbm, white_ref, traces, table, sems):
    channels = white_ref.shape[0]
    stretches = traces.shape[0] // channels
    group = stretches
    table_copy = pltpu.make_async_copy(table_hbm, table, sems.at[stretches])
    table_copy.start()
    copies = [
        pltpu.make_async_copy(
            traces_hbm.at[:, pl.ds(n * step, step)], traces.at[pl.ds(n * channels, channels)], sems.at[n]
        )
        for n in range(stretches)
    ]
    for copy in copies:
        copy.start()
    number = lax.broadcasted_iota(jnp.int32, (stretches, BAND), 0)
    bins = lax.broadcasted_iota(jnp.int32, (stretches, BAND), 1) + BAND_LO
    turn = lax.rem(number * bins, stretches).astype(jnp.float32) * (2.0 * math.pi / stretches)
    turn_cos, turn_sin = jnp.cos(turn), jnp.sin(turn)
    table_copy.wait()
    real = imag = None
    for start in range(0, stretches, group):
        for copy in copies[start : start + group]:
            copy.wait()
        part = traces[start * channels : (start + group) * channels]
        y = jnp.dot(part, table[0], preferred_element_type=jnp.float32)
        y = y + jnp.dot(part, table[1], preferred_element_type=jnp.float32)
        for n in range(group):
            y_real = y[n * channels : (n + 1) * channels, :BAND]
            y_imag = y[n * channels : (n + 1) * channels, BAND:]
            if start + n == 0:
                real, imag = y_real, y_imag
                continue
            cosine, sine = turn_cos[start + n : start + n + 1], turn_sin[start + n : start + n + 1]
            real = real + (y_real * cosine + y_imag * sine)
            imag = imag + (y_imag * cosine - y_real * sine)
    power = real * real + imag * imag
    level = jnp.mean(power, axis=1, keepdims=True)
    denom = jnp.sqrt(power + water_level * level + epsilon)
    white_ref[:, :BAND] = (real / denom).astype(jnp.bfloat16)
    white_ref[:, BAND:] = (imag / denom).astype(jnp.bfloat16)


def spectra(traces):
    channels, samples = traces.shape
    step = 256
    table = split_table(samples, step)
    hbm = pl.BlockSpec(memory_space=pltpu.HBM)
    return pl.pallas_call(
        functools.partial(spectrum_kernel, step),
        out_shape=jax.ShapeDtypeStruct((channels, 2 * BAND), jnp.bfloat16),
        in_specs=[hbm] * 2,
        out_specs=pl.BlockSpec(memory_space=pltpu.VMEM),
        scratch_shapes=[
            pltpu.VMEM((samples // step * channels, step), traces.dtype),
            pltpu.VMEM(table.shape, jnp.bfloat16),
            pltpu.SemaphoreType.DMA((samples // step + 1,)),
        ],
        cost_estimate=pl.CostEstimate(flops=10**9, bytes_accessed=2**20, transcendentals=0),
        compiler_params=pltpu.CompilerParams(vmem_limit_bytes=SPECTRUM_VMEM),
    )(traces, jnp.asarray(table))


def quad_kernel(white_ref, other_ref, across_ref, diagonal_ref, quad_ref):
    half = white_ref.shape[1]
    quad_ref[0, :, :half] = white_ref[...]
    quad_ref[0, :, half:] = other_ref[...]
    quad_ref[1, :, :half] = across_ref[...]
    quad_ref[1, :, half:] = diagonal_ref[...]


def assemble(*quarters):
    channels, depth = quarters[0].shape
    vmem = pl.BlockSpec(memory_space=pltpu.VMEM)
    return pl.pallas_call(
        quad_kernel,
        out_shape=jax.ShapeDtypeStruct((2, channels, 2 * depth), quarters[0].dtype),
        in_specs=[vmem] * 4,
        out_specs=vmem,
        compiler_params=pltpu.CompilerParams(vmem_limit_bytes=2 * 2**20),
        cost_estimate=pl.CostEstimate(flops=10**9, bytes_accessed=2**19, transcendentals=0),
    )(*quarters)


def rows_kernel(samples, norm_scale, pair_ref, partners_ref, rows_ref, scale_ref, stage, own, lag_cos, lag_sin):
    slots = scale_ref.shape[0]
    slot = lax.broadcasted_iota(jnp.int32, (slots, slots), 0) == lax.broadcasted_iota(jnp.int32, (slots, slots), 1)
    factor = jnp.where(slot & (jnp.broadcast_to(partners_ref[...], (slots, slots)) >= 0), norm_scale, 0.0)
    scale_ref[...] = jnp.broadcast_to(jnp.sum(factor, axis=1, keepdims=True), scale_ref.shape)
    lag = lax.broadcasted_iota(jnp.int32, lag_cos.shape, 0)
    bins = lax.broadcasted_iota(jnp.int32, lag_cos.shape, 1) + BAND_LO
    angle = lax.rem((lag + (samples - LAG)) * bins, samples).astype(jnp.float32) * (2.0 * math.pi / samples)
    lag_cos[...] = jnp.cos(angle)
    lag_sin[...] = jnp.sin(angle)
    pairs = own.shape[1]
    first = pl.multiple_of(lax.axis_index("seg") * 2 * pairs, 2 * pairs)
    mine = pair_ref[0, pl.ds(first, 2 * pairs), :].astype(jnp.float32)
    for left in range(0, mine.shape[1], 128):
        stage[...] = mine[:, left : left + 128]
        for member in range(2):
            own[member, :, left : left + 128] = stage[pl.ds(member, pairs, stride=2), :]

    def turn(lag, carry):
        cosine, sine = lag_cos[pl.ds(lag, 1), :], lag_sin[pl.ds(lag, 1), :]
        at = pl.ds(pl.multiple_of(lag * pairs, pairs), pairs)
        for member in range(2):
            for left in range(0, own.shape[2], 2 * BAND):
                middle, right = left + BAND, left + 2 * BAND
                real, imag = own[member, :, left:middle], own[member, :, middle:right]
                rows_ref[member, at, left:middle] = (real * cosine - imag * sine).astype(jnp.bfloat16)
                rows_ref[member, at, middle:right] = (real * sine + imag * cosine).astype(jnp.bfloat16)
        return carry

    lax.fori_loop(0, LAGS, turn, 0, unroll=5)


def multiply(rows_ref, window, scale, tiles, done):
    members = len(scale)
    width = window.shape[0] // members
    lines = rows_ref.shape[1]
    bounds = [lines * cut // 13 // 16 * 16 for cut in (0, 6, 10)] + [lines]
    for number, (low, high) in enumerate(zip(bounds[:-1], bounds[1:])):
        even, odd = [
            lax.dot_general(
                rows_ref[m, low:high], window[...], (((1,), (1,)), ((), ())), preferred_element_type=jnp.float32
            )
            for m in range(2)
        ]
        lane = lax.broadcasted_iota(jnp.int32, (high - low, 2 * width), 1)
        for n in range(0, members, 2):
            a, b = even[:, n * width : (n + 2) * width], odd[:, n * width : (n + 2) * width]
            tiles[n, low:high] = jnp.where(lane < width, a, pltpu.roll(b, width, 1)) * scale[n]
            tiles[n + 1, low:high] = jnp.where(lane < width, pltpu.roll(a, width, 1), b) * scale[n + 1]
        done(number, low, high)


class Sender:
    def __init__(self, tiles, slots, out_ref, sems, last=None):
        self.tiles, self.slots, self.out_ref, self.sems, self.last = tiles, slots, out_ref, sems, last
        self.steady = len(slots) if last is None else len(slots) - 1
        self.sent = []

    def copy(self, number, n, low, high):
        return pltpu.make_async_copy(
            self.tiles.at[n, low:high],
            self.out_ref.at[self.slots[n], low:high],
            self.sems.at[number * len(self.slots) + n],
        )

    def send(self, number, low, high):
        for n in range(self.steady):
            copy = self.copy(number, n, low, high)
            self.sent.append(copy)
            copy.start()

    def send_last(self):
        pl.when(self.last)(self.copy(0, self.steady, 0, self.tiles.shape[1]).start)

    def wait(self):
        for copy in self.sent:
            copy.wait()
        if self.last is not None:
            pl.when(self.last)(self.copy(0, self.steady, 0, self.tiles.shape[1]).wait)


def slot_of(plane, swap_x, swap_core):
    place = lax.rem(lax.axis_index("chan"), QUAD)
    step_x = 2 - 4 * lax.div(place, 2)
    step_core = 1 - 2 * lax.rem(place, 2)
    return REACH + QUAD * plane + swap_x * step_x + swap_core * step_core


def near_kernel(rows_ref, scale_ref, own_ref, sibling_ref, out_ref, window, tiles, sems):
    width = own_ref.shape[1]
    slots = []
    for core, ref in enumerate((own_ref, sibling_ref)):
        for x in range(2):
            n = len(slots)
            window[n * width : (n + 1) * width] = ref[x]
            slots.append(slot_of(0, x, core))
    scale = [scale_ref[pl.ds(slot, 1), :] for slot in slots]
    sender = Sender(tiles, slots, out_ref, sems)
    multiply(rows_ref, window, scale, tiles, sender.send)
    sender.wait()


def far_slots(core):
    chan = lax.axis_index("chan")
    place = lax.rem(chan, QUAD)
    ahead = 2 * lax.rem(lax.div(chan, QUAD), 2) - 1
    side = 1 - 2 * lax.div(place, 2)
    at_end = (place == 0) | (place == QUAD - 1)
    slots = [slot_of(ahead, 0, core), slot_of(-ahead, 0, core), slot_of(-side, 1, core)]
    if core == 0:
        slots.append(jnp.where(place == 0, 0, 2 * REACH))
        return slots, at_end
    slots.append(jnp.clip(slot_of(side, 1, core), 0, 2 * REACH))
    return slots, jnp.logical_not(at_end)


def load_far(first_ref, second_ref, window):
    chan = lax.axis_index("chan")
    width = first_ref.shape[1]
    ahead = 2 * lax.rem(lax.div(chan, QUAD), 2) - 1
    side = 1 - 2 * lax.div(lax.rem(chan, QUAD), 2)
    place = jnp.where(ahead == side, 3, 2)
    window[:width] = first_ref[0]
    window[width : 2 * width] = second_ref[0]
    window[pl.ds(pl.multiple_of(place * width, width), width), :] = first_ref[1]
    window[pl.ds(pl.multiple_of((5 - place) * width, width), width), :] = second_ref[1]


def own_kernel(rows_ref, scale_ref, first_ref, second_ref, corner_ref, tiles_ref, window):
    width = first_ref.shape[1]
    slots, last = far_slots(0)
    load_far(first_ref, second_ref, window)

    @pl.when(last)
    def _():
        window[3 * width :] = corner_ref[...]

    scale = [scale_ref[pl.ds(slot, 1), :] for slot in slots]
    multiply(rows_ref, window, scale, tiles_ref, lambda *stretch: None)


def sibling_kernel(rows_ref, scale_ref, first_ref, second_ref, own_tiles_ref, near_ref, out_ref, window, tiles, sems,
                   own_sems):
    del near_ref
    own_slots, own_last = far_slots(0)
    own_sender = Sender(own_tiles_ref, own_slots, out_ref, own_sems, own_last)
    own_sender.send(0, 0, own_tiles_ref.shape[1])
    own_sender.send_last()
    slots, last = far_slots(1)
    load_far(first_ref, second_ref, window)
    scale = [scale_ref[pl.ds(slot, 1), :] for slot in slots]
    sender = Sender(tiles, slots, out_ref, sems, last)
    multiply(rows_ref, window, scale, tiles, sender.send)
    sender.send_last()
    own_sender.wait()
    sender.wait()


def lag_rows(quad, partners, samples, half, norm_scale):
    width, depth = quad.shape[1:]
    vmem = pl.BlockSpec(memory_space=pltpu.VMEM)
    return pl.pallas_call(
        functools.partial(rows_kernel, samples, norm_scale),
        out_shape=[
            jax.ShapeDtypeStruct((2, LAGS * half // 2, depth), jnp.bfloat16),
            jax.ShapeDtypeStruct((partners.shape[1], 2 * width), jnp.float32),
        ],
        in_specs=[vmem, vmem],
        out_specs=[vmem, vmem],
        scratch_shapes=[
            pltpu.VMEM((half, 128), jnp.float32),
            pltpu.VMEM((2, half // 2, depth), jnp.float32),
            pltpu.VMEM((LAGS, BAND), jnp.float32),
            pltpu.VMEM((LAGS, BAND), jnp.float32),
        ],
        compiler_params=pltpu.CompilerParams(vmem_limit_bytes=KERNEL_VMEM),
        cost_estimate=pl.CostEstimate(flops=5 * 10**9, bytes_accessed=2**20, transcendentals=0),
    )(quad, partners)


def correlate(kernel, operands, out=None, tiles_only=False):
    rows, scale, blobs = operands[:3]
    width, depth = blobs.shape[-2:]
    lines = rows.shape[1]
    vmem = pl.BlockSpec(memory_space=pltpu.VMEM)
    anywhere = pl.BlockSpec(memory_space=pl.ANY)
    extra = [] if out is None else [out]
    scratch = [pltpu.VMEM((QUAD * width, depth), jnp.bfloat16)]
    if not tiles_only:
        scratch += [pltpu.VMEM((QUAD, lines, 2 * width), jnp.float32), pltpu.SemaphoreType.DMA((3 * QUAD,))]
    if extra:
        scratch += [pltpu.SemaphoreType.DMA((QUAD,))]
    return pl.pallas_call(
        kernel,
        out_shape=jax.ShapeDtypeStruct((QUAD if tiles_only else scale.shape[0], lines, 2 * width), jnp.float32),
        in_specs=[vmem] * len(operands) + [anywhere] * len(extra),
        out_specs=vmem if tiles_only else anywhere,
        scratch_shapes=scratch,
        input_output_aliases={len(operands): 0} if extra else {},
        compiler_params=pltpu.CompilerParams(vmem_limit_bytes=KERNEL_VMEM),
        cost_estimate=pl.CostEstimate(
            flops=4 * lines * depth * QUAD * width, bytes_accessed=8 * QUAD * lines * width, transcendentals=0
        ),
    )(*operands, *extra)


def local(traces, partners):
    slots = partners.shape[1]
    segments = lax.axis_size("seg")
    blocks = lax.axis_size("chan")
    channels = traces.shape[1]
    half = channels // segments
    assert segments == 2 and blocks % QUAD == 0 and slots == 2 * REACH + 1
    plane_two = [(c, c ^ QUAD) for c in range(blocks)]
    plane_one = [(c, ((c + QUAD) ^ QUAD) - QUAD) for c in range(QUAD, blocks - QUAD)]
    sibling = [(c, c ^ 1) for c in range(blocks)]
    corners = [(c, c + REACH) for c in range(QUAD - 1, blocks - REACH, QUAD)]
    corners += [(c, c - REACH) for c in range(2 * QUAD, blocks, QUAD)]
    norm_scale = (segments * BAND) ** (-0.5)
    white = spectra(traces[0])
    corner = lax.ppermute(white, "chan", corners)
    other = lax.ppermute(white, "seg", [(0, 1), (1, 0)])
    across = lax.ppermute(white, "chan", [(c, c ^ 2) for c in range(blocks)])
    diagonal = [(s * blocks + c, (1 - s) * blocks + (c ^ 2)) for s in range(segments) for c in range(blocks)]
    diagonal = lax.ppermute(white, ("seg", "chan"), diagonal)
    quad = assemble(white, other, across, diagonal)
    first = lax.ppermute(quad, "chan", plane_one)
    second = lax.ppermute(quad, "chan", plane_two)
    near, corner = lax.optimization_barrier((quad, corner))
    corner_other = lax.ppermute(corner, "seg", [(0, 1), (1, 0)])
    beside = lax.ppermute(near, "chan", sibling)
    rows, scale = lag_rows(near, partners, traces.shape[2], half, norm_scale)
    out = correlate(near_kernel, [rows, scale, quad, beside])
    corner = jnp.concatenate([corner, corner_other], axis=1)
    first, second, out = lax.optimization_barrier((first, second, out))
    sib_first = lax.ppermute(first, "chan", sibling)
    sib_second = lax.ppermute(second, "chan", sibling)
    tiles = correlate(own_kernel, [rows, scale, first, second, corner], tiles_only=True)
    out = correlate(sibling_kernel, [rows, scale, sib_first, sib_second, tiles], out)
    return out.reshape(1, slots, LAGS, half * channels)


def solution(mesh):
    placed = (P("seg", "chan", None), P("chan", None))
    return jax.shard_map(
        local, mesh=mesh, in_specs=placed, out_specs=P("chan", None, None, "seg"), check_vma=False
    )
```

```python
import functools
import math

import jax
import jax.numpy as jnp
import numpy as np
from jax import lax
from jax.experimental import pallas as pl
from jax.experimental.pallas import tpu as pltpu
from jax.sharding import PartitionSpec as P

BAND = 256
BAND_LO = 16
LAG = 32
LAGS = 2 * LAG + 1
REACH = 5
QUAD = 4
SPECTRUM_VMEM = 55040 * 2**10
KERNEL_VMEM = 24 * 2**20

water_level = 0.5
epsilon = 1e-06


def split_table(samples, step):
    bins = np.arange(BAND) + BAND_LO
    angle = (np.arange(step)[:, None] * bins[None, :] % samples) * (2.0 * math.pi / samples)
    table = np.concatenate([np.cos(angle), -np.sin(angle)], axis=1).astype(np.float32)
    high = table.astype(jnp.bfloat16)
    low = (table - high.astype(np.float32)).astype(jnp.bfloat16)
    return np.stack([high, low])


def spectrum_kernel(step, traces_hbm, table_hbm, white_ref, traces, table, sems):
    channels = white_ref.shape[0]
    stretches = traces.shape[0] // channels
    group = stretches
    table_copy = pltpu.make_async_copy(table_hbm, table, sems.at[stretches])
    table_copy.start()
    copies = [
        pltpu.make_async_copy(
            traces_hbm.at[:, pl.ds(n * step, step)], traces.at[pl.ds(n * channels, channels)], sems.at[n]
        )
        for n in range(stretches)
    ]
    for copy in copies:
        copy.start()
    number = lax.broadcasted_iota(jnp.int32, (stretches, BAND), 0)
    bins = lax.broadcasted_iota(jnp.int32, (stretches, BAND), 1) + BAND_LO
    turn = lax.rem(number * bins, stretches).astype(jnp.float32) * (2.0 * math.pi / stretches)
    turn_cos, turn_sin = jnp.cos(turn), jnp.sin(turn)
    table_copy.wait()
    real = imag = None
    for start in range(0, stretches, group):
        for copy in copies[start : start + group]:
            copy.wait()
        part = traces[start * channels : (start + group) * channels]
        y = jnp.dot(part, table[0], preferred_element_type=jnp.float32)
        y = y + jnp.dot(part, table[1], preferred_element_type=jnp.float32)
        for n in range(group):
            y_real = y[n * channels : (n + 1) * channels, :BAND]
            y_imag = y[n * channels : (n + 1) * channels, BAND:]
            if start + n == 0:
                real, imag = y_real, y_imag
                continue
            cosine, sine = turn_cos[start + n : start + n + 1], turn_sin[start + n : start + n + 1]
            real = real + (y_real * cosine + y_imag * sine)
            imag = imag + (y_imag * cosine - y_real * sine)
    power = real * real + imag * imag
    level = jnp.mean(power, axis=1, keepdims=True)
    denom = jnp.sqrt(power + water_level * level + epsilon)
    white_ref[:, :BAND] = (real / denom).astype(jnp.bfloat16)
    white_ref[:, BAND:] = (imag / denom).astype(jnp.bfloat16)


def spectra(traces):
    channels, samples = traces.shape
    step = 256
    table = split_table(samples, step)
    hbm = pl.BlockSpec(memory_space=pltpu.HBM)
    return pl.pallas_call(
        functools.partial(spectrum_kernel, step),
        out_shape=jax.ShapeDtypeStruct((channels, 2 * BAND), jnp.bfloat16),
        in_specs=[hbm] * 2,
        out_specs=pl.BlockSpec(memory_space=pltpu.VMEM),
        scratch_shapes=[
            pltpu.VMEM((samples // step * channels, step), traces.dtype),
            pltpu.VMEM(table.shape, jnp.bfloat16),
            pltpu.SemaphoreType.DMA((samples // step + 1,)),
        ],
        cost_estimate=pl.CostEstimate(flops=10**9, bytes_accessed=2**20, transcendentals=0),
        compiler_params=pltpu.CompilerParams(vmem_limit_bytes=SPECTRUM_VMEM),
    )(traces, jnp.asarray(table))


def quad_kernel(white_ref, other_ref, across_ref, diagonal_ref, quad_ref):
    half = white_ref.shape[1]
    quad_ref[0, :, :half] = white_ref[...]
    quad_ref[0, :, half:] = other_ref[...]
    quad_ref[1, :, :half] = across_ref[...]
    quad_ref[1, :, half:] = diagonal_ref[...]


def assemble(*quarters):
    channels, depth = quarters[0].shape
    vmem = pl.BlockSpec(memory_space=pltpu.VMEM)
    return pl.pallas_call(
        quad_kernel,
        out_shape=jax.ShapeDtypeStruct((2, channels, 2 * depth), quarters[0].dtype),
        in_specs=[vmem] * 4,
        out_specs=vmem,
        compiler_params=pltpu.CompilerParams(vmem_limit_bytes=2 * 2**20),
        cost_estimate=pl.CostEstimate(flops=10**9, bytes_accessed=2**19, transcendentals=0),
    )(*quarters)


def rows_kernel(samples, norm_scale, pair_ref, partners_ref, rows_ref, scale_ref, stage, own, lag_cos, lag_sin):
    slots = scale_ref.shape[0]
    slot = lax.broadcasted_iota(jnp.int32, (slots, slots), 0) == lax.broadcasted_iota(jnp.int32, (slots, slots), 1)
    factor = jnp.where(slot & (jnp.broadcast_to(partners_ref[...], (slots, slots)) >= 0), norm_scale, 0.0)
    scale_ref[...] = jnp.broadcast_to(jnp.sum(factor, axis=1, keepdims=True), scale_ref.shape)
    lag = lax.broadcasted_iota(jnp.int32, lag_cos.shape, 0)
    bins = lax.broadcasted_iota(jnp.int32, lag_cos.shape, 1) + BAND_LO
    angle = lax.rem((lag + (samples - LAG)) * bins, samples).astype(jnp.float32) * (2.0 * math.pi / samples)
    lag_cos[...] = jnp.cos(angle)
    lag_sin[...] = jnp.sin(angle)
    pairs = own.shape[1]
    first = pl.multiple_of(lax.axis_index("seg") * 2 * pairs, 2 * pairs)
    mine = pair_ref[0, pl.ds(first, 2 * pairs), :].astype(jnp.float32)
    for left in range(0, mine.shape[1], 128):
        stage[...] = mine[:, left : left + 128]
        for member in range(2):
            own[member, :, left : left + 128] = stage[pl.ds(member, pairs, stride=2), :]

    def turn(lag, carry):
        cosine, sine = lag_cos[pl.ds(lag, 1), :], lag_sin[pl.ds(lag, 1), :]
        at = pl.ds(pl.multiple_of(lag * pairs, pairs), pairs)
        for member in range(2):
            for left in range(0, own.shape[2], 2 * BAND):
                middle, right = left + BAND, left + 2 * BAND
                real, imag = own[member, :, left:middle], own[member, :, middle:right]
                rows_ref[member, at, left:middle] = (real * cosine - imag * sine).astype(jnp.bfloat16)
                rows_ref[member, at, middle:right] = (real * sine + imag * cosine).astype(jnp.bfloat16)
        return carry

    lax.fori_loop(0, LAGS, turn, 0, unroll=5)


def multiply(rows_ref, window, scale, tiles, done):
    members = len(scale)
    width = window.shape[0] // members
    lines = rows_ref.shape[1]
    bounds = [lines * cut // 13 // 16 * 16 for cut in (0, 6, 10)] + [lines]
    for number, (low, high) in enumerate(zip(bounds[:-1], bounds[1:])):
        even, odd = [
            lax.dot_general(
                rows_ref[m, low:high], window[...], (((1,), (1,)), ((), ())), preferred_element_type=jnp.float32
            )
            for m in range(2)
        ]
        lane = lax.broadcasted_iota(jnp.int32, (high - low, 2 * width), 1)
        for n in range(0, members, 2):
            a, b = even[:, n * width : (n + 2) * width], odd[:, n * width : (n + 2) * width]
            tiles[n, low:high] = jnp.where(lane < width, a, pltpu.roll(b, width, 1)) * scale[n]
            tiles[n + 1, low:high] = jnp.where(lane < width, pltpu.roll(a, width, 1), b) * scale[n + 1]
        done(number, low, high)


class Sender:
    def __init__(self, tiles, slots, out_ref, sems):
        self.tiles, self.slots, self.out_ref, self.sems = tiles, slots, out_ref, sems
        self.sent = []

    def send(self, number, low, high):
        for n, slot in enumerate(self.slots):
            copy = pltpu.make_async_copy(
                self.tiles.at[n, low:high],
                self.out_ref.at[slot, low:high],
                self.sems.at[number * len(self.slots) + n],
            )
            self.sent.append(copy)
            copy.start()

    def wait(self):
        for copy in self.sent:
            copy.wait()


def slot_of(plane, swap_x, swap_core):
    place = lax.rem(lax.axis_index("chan"), QUAD)
    step_x = 2 - 4 * lax.div(place, 2)
    step_core = 1 - 2 * lax.rem(place, 2)
    return REACH + QUAD * plane + swap_x * step_x + swap_core * step_core


def near_kernel(rows_ref, scale_ref, own_ref, sibling_ref, out_ref, window, tiles, sems):
    width = own_ref.shape[1]
    slots = []
    for core, ref in enumerate((own_ref, sibling_ref)):
        for x in range(2):
            n = len(slots)
            window[n * width : (n + 1) * width] = ref[x]
            slots.append(slot_of(0, x, core))
    scale = [scale_ref[pl.ds(slot, 1), :] for slot in slots]
    sender = Sender(tiles, slots, out_ref, sems)
    multiply(rows_ref, window, scale, tiles, sender.send)
    sender.wait()


def far_slots(core):
    chan = lax.axis_index("chan")
    place = lax.rem(chan, QUAD)
    ahead = 2 * lax.rem(lax.div(chan, QUAD), 2) - 1
    side = 1 - 2 * lax.div(place, 2)
    last = jnp.clip(slot_of(side, 1, core), 0, 2 * REACH)
    if core == 1:
        last = jnp.where(place == 0, 0, jnp.where(place == QUAD - 1, 2 * REACH, last))
    slots = [slot_of(ahead, 0, core), slot_of(-ahead, 0, core), slot_of(-side, 1, core), last]
    return slots, (place == 0) | (place == QUAD - 1)


def load_far(first_ref, second_ref, window):
    chan = lax.axis_index("chan")
    width = first_ref.shape[1]
    ahead = 2 * lax.rem(lax.div(chan, QUAD), 2) - 1
    side = 1 - 2 * lax.div(lax.rem(chan, QUAD), 2)
    place = jnp.where(ahead == side, 3, 2)
    window[:width] = first_ref[0]
    window[width : 2 * width] = second_ref[0]
    window[pl.ds(pl.multiple_of(place * width, width), width), :] = first_ref[1]
    window[pl.ds(pl.multiple_of((5 - place) * width, width), width), :] = second_ref[1]


def own_kernel(rows_ref, scale_ref, first_ref, second_ref, tiles_ref, window):
    slots, _ = far_slots(0)
    load_far(first_ref, second_ref, window)
    scale = [scale_ref[pl.ds(slot, 1), :] for slot in slots]
    multiply(rows_ref, window, scale, tiles_ref, lambda *stretch: None)


def sibling_kernel(rows_ref, scale_ref, first_ref, second_ref, corner_ref, own_tiles_ref, near_ref, out_ref, window, tiles,
                   sems, own_sems):
    del near_ref
    own_sender = Sender(own_tiles_ref, far_slots(0)[0][:3], out_ref, own_sems)
    own_sender.send(0, 0, own_tiles_ref.shape[1])
    slots, stands = far_slots(1)
    load_far(first_ref, second_ref, window)

    @pl.when(stands)
    def _():
        window[3 * first_ref.shape[1] :] = corner_ref[...]

    scale = [scale_ref[pl.ds(slot, 1), :] for slot in slots]
    sender = Sender(tiles, slots, out_ref, sems)
    multiply(rows_ref, window, scale, tiles, sender.send)
    own_sender.wait()
    sender.wait()


def lag_rows(quad, partners, samples, half, norm_scale):
    width, depth = quad.shape[1:]
    vmem = pl.BlockSpec(memory_space=pltpu.VMEM)
    return pl.pallas_call(
        functools.partial(rows_kernel, samples, norm_scale),
        out_shape=[
            jax.ShapeDtypeStruct((2, LAGS * half // 2, depth), jnp.bfloat16),
            jax.ShapeDtypeStruct((partners.shape[1], 2 * width), jnp.float32),
        ],
        in_specs=[vmem, vmem],
        out_specs=[vmem, vmem],
        scratch_shapes=[
            pltpu.VMEM((half, 128), jnp.float32),
            pltpu.VMEM((2, half // 2, depth), jnp.float32),
            pltpu.VMEM((LAGS, BAND), jnp.float32),
            pltpu.VMEM((LAGS, BAND), jnp.float32),
        ],
        compiler_params=pltpu.CompilerParams(vmem_limit_bytes=KERNEL_VMEM),
        cost_estimate=pl.CostEstimate(flops=5 * 10**9, bytes_accessed=2**20, transcendentals=0),
    )(quad, partners)


def correlate(kernel, operands, out=None, tiles_only=False):
    rows, scale, blobs = operands[:3]
    width, depth = blobs.shape[-2:]
    lines = rows.shape[1]
    vmem = pl.BlockSpec(memory_space=pltpu.VMEM)
    anywhere = pl.BlockSpec(memory_space=pl.ANY)
    extra = [] if out is None else [out]
    scratch = [pltpu.VMEM((QUAD * width, depth), jnp.bfloat16)]
    if not tiles_only:
        scratch += [pltpu.VMEM((QUAD, lines, 2 * width), jnp.float32), pltpu.SemaphoreType.DMA((3 * QUAD,))]
    if extra:
        scratch += [pltpu.SemaphoreType.DMA((QUAD,))]
    return pl.pallas_call(
        kernel,
        out_shape=jax.ShapeDtypeStruct((QUAD if tiles_only else scale.shape[0], lines, 2 * width), jnp.float32),
        in_specs=[vmem] * len(operands) + [anywhere] * len(extra),
        out_specs=vmem if tiles_only else anywhere,
        scratch_shapes=scratch,
        input_output_aliases={len(operands): 0} if extra else {},
        compiler_params=pltpu.CompilerParams(vmem_limit_bytes=KERNEL_VMEM),
        cost_estimate=pl.CostEstimate(
            flops=4 * lines * depth * QUAD * width, bytes_accessed=8 * QUAD * lines * width, transcendentals=0
        ),
    )(*operands, *extra)


def local(traces, partners):
    slots = partners.shape[1]
    segments = lax.axis_size("seg")
    blocks = lax.axis_size("chan")
    channels = traces.shape[1]
    half = channels // segments
    assert segments == 2 and blocks % QUAD == 0 and slots == 2 * REACH + 1
    plane_two = [(c, c ^ QUAD) for c in range(blocks)]
    plane_one = [(c, ((c + QUAD) ^ QUAD) - QUAD) for c in range(QUAD, blocks - QUAD)]
    sibling = [(c, c ^ 1) for c in range(blocks)]
    corners = [(c, c + REACH) for c in range(QUAD - 1, blocks - REACH, QUAD)]
    corners += [(c, c - REACH) for c in range(2 * QUAD, blocks, QUAD)]
    norm_scale = (segments * BAND) ** (-0.5)
    white = spectra(traces[0])
    corner = lax.ppermute(white, "chan", corners)
    other = lax.ppermute(white, "seg", [(0, 1), (1, 0)])
    across = lax.ppermute(white, "chan", [(c, c ^ 2) for c in range(blocks)])
    diagonal = [(s * blocks + c, (1 - s) * blocks + (c ^ 2)) for s in range(segments) for c in range(blocks)]
    diagonal = lax.ppermute(white, ("seg", "chan"), diagonal)
    quad = assemble(white, other, across, diagonal)
    first = lax.ppermute(quad, "chan", plane_one)
    second = lax.ppermute(quad, "chan", plane_two)
    near, corner = lax.optimization_barrier((quad, corner))
    corner_other = lax.ppermute(corner, "seg", [(0, 1), (1, 0)])
    beside = lax.ppermute(near, "chan", sibling)
    rows, scale = lag_rows(near, partners, traces.shape[2], half, norm_scale)
    out = correlate(near_kernel, [rows, scale, quad, beside])
    corner = jnp.concatenate([corner, corner_other], axis=1)
    first, second, out = lax.optimization_barrier((first, second, out))
    sib_first = lax.ppermute(first, "chan", sibling)
    sib_second = lax.ppermute(second, "chan", sibling)
    tiles = correlate(own_kernel, [rows, scale, first, second], tiles_only=True)
    out = correlate(sibling_kernel, [rows, scale, sib_first, sib_second, corner, tiles], out)
    return out.reshape(1, slots, LAGS, half * channels)


def solution(mesh):
    placed = (P("seg", "chan", None), P("chan", None))
    return jax.shard_map(
        local, mesh=mesh, in_specs=placed, out_specs=P("chan", None, None, "seg"), check_vma=False
    )
```

```python
import functools
import math

import jax
import jax.numpy as jnp
import numpy as np
from jax import lax
from jax.experimental import pallas as pl
from jax.experimental.pallas import tpu as pltpu
from jax.sharding import PartitionSpec as P

BAND = 256
BAND_LO = 16
LAG = 32
LAGS = 2 * LAG + 1
REACH = 5
QUAD = 4
SPECTRUM_VMEM = 55040 * 2**10
KERNEL_VMEM = 24 * 2**20

water_level = 0.5
epsilon = 1e-06


def split_table(samples, step):
    bins = np.arange(BAND) + BAND_LO
    angle = (np.arange(step)[:, None] * bins[None, :] % samples) * (2.0 * math.pi / samples)
    table = np.concatenate([np.cos(angle), -np.sin(angle)], axis=1).astype(np.float32)
    high = table.astype(jnp.bfloat16)
    low = (table - high.astype(np.float32)).astype(jnp.bfloat16)
    return np.stack([high, low])


def spectrum_kernel(step, traces_hbm, table_hbm, white_ref, traces, table, sems):
    channels = white_ref.shape[0]
    stretches = traces.shape[0] // channels
    group = stretches
    table_copy = pltpu.make_async_copy(table_hbm, table, sems.at[stretches])
    table_copy.start()
    copies = [
        pltpu.make_async_copy(
            traces_hbm.at[:, pl.ds(n * step, step)], traces.at[pl.ds(n * channels, channels)], sems.at[n]
        )
        for n in range(stretches)
    ]
    for copy in copies:
        copy.start()
    number = lax.broadcasted_iota(jnp.int32, (stretches, BAND), 0)
    bins = lax.broadcasted_iota(jnp.int32, (stretches, BAND), 1) + BAND_LO
    turn = lax.rem(number * bins, stretches).astype(jnp.float32) * (2.0 * math.pi / stretches)
    turn_cos, turn_sin = jnp.cos(turn), jnp.sin(turn)
    table_copy.wait()
    real = imag = None
    for start in range(0, stretches, group):
        for copy in copies[start : start + group]:
            copy.wait()
        part = traces[start * channels : (start + group) * channels]
        y = jnp.dot(part, table[0], preferred_element_type=jnp.float32)
        y = y + jnp.dot(part, table[1], preferred_element_type=jnp.float32)
        for n in range(group):
            y_real = y[n * channels : (n + 1) * channels, :BAND]
            y_imag = y[n * channels : (n + 1) * channels, BAND:]
            if start + n == 0:
                real, imag = y_real, y_imag
                continue
            cosine, sine = turn_cos[start + n : start + n + 1], turn_sin[start + n : start + n + 1]
            real = real + (y_real * cosine + y_imag * sine)
            imag = imag + (y_imag * cosine - y_real * sine)
    power = real * real + imag * imag
    level = jnp.mean(power, axis=1, keepdims=True)
    denom = jnp.sqrt(power + water_level * level + epsilon)
    white_ref[:, :BAND] = (real / denom).astype(jnp.bfloat16)
    white_ref[:, BAND:] = (imag / denom).astype(jnp.bfloat16)


def spectra(traces):
    channels, samples = traces.shape
    step = 256
    table = split_table(samples, step)
    hbm = pl.BlockSpec(memory_space=pltpu.HBM)
    return pl.pallas_call(
        functools.partial(spectrum_kernel, step),
        out_shape=jax.ShapeDtypeStruct((channels, 2 * BAND), jnp.bfloat16),
        in_specs=[hbm] * 2,
        out_specs=pl.BlockSpec(memory_space=pltpu.VMEM),
        scratch_shapes=[
            pltpu.VMEM((samples // step * channels, step), traces.dtype),
            pltpu.VMEM(table.shape, jnp.bfloat16),
            pltpu.SemaphoreType.DMA((samples // step + 1,)),
        ],
        cost_estimate=pl.CostEstimate(flops=10**9, bytes_accessed=2**20, transcendentals=0),
        compiler_params=pltpu.CompilerParams(vmem_limit_bytes=SPECTRUM_VMEM),
    )(traces, jnp.asarray(table))


def quad_kernel(white_ref, other_ref, across_ref, diagonal_ref, quad_ref):
    half = white_ref.shape[1]
    quad_ref[0, :, :half] = white_ref[...]
    quad_ref[0, :, half:] = other_ref[...]
    quad_ref[1, :, :half] = across_ref[...]
    quad_ref[1, :, half:] = diagonal_ref[...]


def assemble(*quarters):
    channels, depth = quarters[0].shape
    vmem = pl.BlockSpec(memory_space=pltpu.VMEM)
    return pl.pallas_call(
        quad_kernel,
        out_shape=jax.ShapeDtypeStruct((2, channels, 2 * depth), quarters[0].dtype),
        in_specs=[vmem] * 4,
        out_specs=vmem,
        compiler_params=pltpu.CompilerParams(vmem_limit_bytes=2 * 2**20),
        cost_estimate=pl.CostEstimate(flops=10**9, bytes_accessed=2**19, transcendentals=0),
    )(*quarters)


def rows_kernel(samples, norm_scale, pair_ref, partners_ref, rows_ref, scale_ref, stage, own, lag_cos, lag_sin):
    slots = scale_ref.shape[0]
    slot = lax.broadcasted_iota(jnp.int32, (slots, slots), 0) == lax.broadcasted_iota(jnp.int32, (slots, slots), 1)
    factor = jnp.where(slot & (jnp.broadcast_to(partners_ref[...], (slots, slots)) >= 0), norm_scale, 0.0)
    scale_ref[...] = jnp.broadcast_to(jnp.sum(factor, axis=1, keepdims=True), scale_ref.shape)
    lag = lax.broadcasted_iota(jnp.int32, lag_cos.shape, 0)
    bins = lax.broadcasted_iota(jnp.int32, lag_cos.shape, 1) + BAND_LO
    angle = lax.rem((lag + (samples - LAG)) * bins, samples).astype(jnp.float32) * (2.0 * math.pi / samples)
    lag_cos[...] = jnp.cos(angle)
    lag_sin[...] = jnp.sin(angle)
    pairs = own.shape[1]
    first = pl.multiple_of(lax.axis_index("seg") * 2 * pairs, 2 * pairs)
    mine = pair_ref[0, pl.ds(first, 2 * pairs), :].astype(jnp.float32)
    for left in range(0, mine.shape[1], 128):
        stage[...] = mine[:, left : left + 128]
        for member in range(2):
            own[member, :, left : left + 128] = stage[pl.ds(member, pairs, stride=2), :]

    def turn(lag, carry):
        cosine, sine = lag_cos[pl.ds(lag, 1), :], lag_sin[pl.ds(lag, 1), :]
        at = pl.ds(pl.multiple_of(lag * pairs, pairs), pairs)
        for member in range(2):
            for left in range(0, own.shape[2], 2 * BAND):
                middle, right = left + BAND, left + 2 * BAND
                real, imag = own[member, :, left:middle], own[member, :, middle:right]
                rows_ref[member, at, left:middle] = (real * cosine - imag * sine).astype(jnp.bfloat16)
                rows_ref[member, at, middle:right] = (real * sine + imag * cosine).astype(jnp.bfloat16)
        return carry

    lax.fori_loop(0, LAGS, turn, 0, unroll=5)


def multiply(rows_ref, window, scale, tiles, done):
    members = len(scale)
    width = window.shape[0] // members
    lines = rows_ref.shape[1]
    bounds = [lines * cut // 13 // 16 * 16 for cut in (0, 6, 10)] + [lines]
    for number, (low, high) in enumerate(zip(bounds[:-1], bounds[1:])):
        even, odd = [
            lax.dot_general(
                rows_ref[m, low:high], window[...], (((1,), (1,)), ((), ())), preferred_element_type=jnp.float32
            )
            for m in range(2)
        ]
        lane = lax.broadcasted_iota(jnp.int32, (high - low, 2 * width), 1)
        for n in range(0, members, 2):
            a, b = even[:, n * width : (n + 2) * width], odd[:, n * width : (n + 2) * width]
            tiles[n, low:high] = jnp.where(lane < width, a, pltpu.roll(b, width, 1)) * scale[n]
            tiles[n + 1, low:high] = jnp.where(lane < width, pltpu.roll(a, width, 1), b) * scale[n + 1]
        done(number, low, high)


class Sender:
    def __init__(self, tiles, slots, out_ref, sems):
        self.tiles, self.slots, self.out_ref, self.sems = tiles, slots, out_ref, sems
        self.sent = []

    def send(self, number, low, high):
        for n, slot in enumerate(self.slots):
            copy = pltpu.make_async_copy(
                self.tiles.at[n, low:high],
                self.out_ref.at[slot, low:high],
                self.sems.at[number * len(self.slots) + n],
            )
            self.sent.append(copy)
            copy.start()

    def wait(self):
        for copy in self.sent:
            copy.wait()


def slot_of(plane, swap_x, swap_core):
    place = lax.rem(lax.axis_index("chan"), QUAD)
    step_x = 2 - 4 * lax.div(place, 2)
    step_core = 1 - 2 * lax.rem(place, 2)
    return REACH + QUAD * plane + swap_x * step_x + swap_core * step_core


def near_kernel(rows_ref, scale_ref, own_ref, sibling_ref, out_ref, window, tiles, sems):
    width = own_ref.shape[1]
    slots = []
    for core, ref in enumerate((own_ref, sibling_ref)):
        for x in range(2):
            n = len(slots)
            window[n * width : (n + 1) * width] = ref[x]
            slots.append(slot_of(0, x, core))
    scale = [scale_ref[pl.ds(slot, 1), :] for slot in slots]
    sender = Sender(tiles, slots, out_ref, sems)
    multiply(rows_ref, window, scale, tiles, sender.send)
    sender.wait()


def far_slots(core):
    chan = lax.axis_index("chan")
    place = lax.rem(chan, QUAD)
    ahead = 2 * lax.rem(lax.div(chan, QUAD), 2) - 1
    side = 1 - 2 * lax.div(place, 2)
    last = jnp.clip(slot_of(side, 1, core), 0, 2 * REACH)
    if core == 1:
        last = jnp.where(place == 0, 0, jnp.where(place == QUAD - 1, 2 * REACH, last))
    slots = [slot_of(ahead, 0, core), slot_of(-ahead, 0, core), slot_of(-side, 1, core), last]
    return slots, (place == 0) | (place == QUAD - 1)


def load_far(first_ref, second_ref, window):
    chan = lax.axis_index("chan")
    width = first_ref.shape[1]
    ahead = 2 * lax.rem(lax.div(chan, QUAD), 2) - 1
    side = 1 - 2 * lax.div(lax.rem(chan, QUAD), 2)
    place = jnp.where(ahead == side, 3, 2)
    window[:width] = first_ref[0]
    window[width : 2 * width] = second_ref[0]
    window[pl.ds(pl.multiple_of(place * width, width), width), :] = first_ref[1]
    window[pl.ds(pl.multiple_of((5 - place) * width, width), width), :] = second_ref[1]


def own_kernel(rows_ref, scale_ref, first_ref, second_ref, tiles_ref, window):
    slots, _ = far_slots(0)
    load_far(first_ref, second_ref, window)
    scale = [scale_ref[pl.ds(slot, 1), :] for slot in slots]
    multiply(rows_ref, window, scale, tiles_ref, lambda *stretch: None)


def sibling_kernel(rows_ref, scale_ref, first_ref, second_ref, corner_ref, own_tiles_ref, near_ref, out_ref, window, tiles,
                   sems, own_sems):
    del near_ref
    own_sender = Sender(own_tiles_ref, far_slots(0)[0][:3], out_ref, own_sems)
    own_sender.send(0, 0, own_tiles_ref.shape[1])
    slots, stands = far_slots(1)
    load_far(first_ref, second_ref, window)

    @pl.when(stands)
    def _():
        window[3 * first_ref.shape[1] :] = corner_ref[...]

    scale = [scale_ref[pl.ds(slot, 1), :] for slot in slots]
    sender = Sender(tiles, slots, out_ref, sems)
    multiply(rows_ref, window, scale, tiles, sender.send)
    own_sender.wait()
    sender.wait()


def lag_rows(quad, partners, samples, half, norm_scale):
    width, depth = quad.shape[1:]
    vmem = pl.BlockSpec(memory_space=pltpu.VMEM)
    return pl.pallas_call(
        functools.partial(rows_kernel, samples, norm_scale),
        out_shape=[
            jax.ShapeDtypeStruct((2, LAGS * half // 2, depth), jnp.bfloat16),
            jax.ShapeDtypeStruct((partners.shape[1], 2 * width), jnp.float32),
        ],
        in_specs=[vmem, vmem],
        out_specs=[vmem, vmem],
        scratch_shapes=[
            pltpu.VMEM((half, 128), jnp.float32),
            pltpu.VMEM((2, half // 2, depth), jnp.float32),
            pltpu.VMEM((LAGS, BAND), jnp.float32),
            pltpu.VMEM((LAGS, BAND), jnp.float32),
        ],
        compiler_params=pltpu.CompilerParams(vmem_limit_bytes=KERNEL_VMEM),
        cost_estimate=pl.CostEstimate(flops=5 * 10**9, bytes_accessed=2**20, transcendentals=0),
    )(quad, partners)


def correlate(kernel, operands, out=None, tiles_only=False):
    rows, scale, blobs = operands[:3]
    width, depth = blobs.shape[-2:]
    lines = rows.shape[1]
    vmem = pl.BlockSpec(memory_space=pltpu.VMEM)
    anywhere = pl.BlockSpec(memory_space=pl.ANY)
    extra = [] if out is None else [out]
    scratch = [pltpu.VMEM((QUAD * width, depth), jnp.bfloat16)]
    if not tiles_only:
        scratch += [pltpu.VMEM((QUAD, lines, 2 * width), jnp.float32), pltpu.SemaphoreType.DMA((3 * QUAD,))]
    if extra:
        scratch += [pltpu.SemaphoreType.DMA((QUAD,))]
    return pl.pallas_call(
        kernel,
        out_shape=jax.ShapeDtypeStruct((QUAD if tiles_only else scale.shape[0], lines, 2 * width), jnp.float32),
        in_specs=[vmem] * len(operands) + [anywhere] * len(extra),
        out_specs=vmem if tiles_only else anywhere,
        scratch_shapes=scratch,
        input_output_aliases={len(operands): 0} if extra else {},
        compiler_params=pltpu.CompilerParams(vmem_limit_bytes=KERNEL_VMEM),
        cost_estimate=pl.CostEstimate(
            flops=4 * lines * depth * QUAD * width, bytes_accessed=8 * QUAD * lines * width, transcendentals=0
        ),
    )(*operands, *extra)


def local(traces, partners):
    slots = partners.shape[1]
    segments = lax.axis_size("seg")
    blocks = lax.axis_size("chan")
    channels = traces.shape[1]
    half = channels // segments
    assert segments == 2 and blocks % QUAD == 0 and slots == 2 * REACH + 1
    plane_two = [(c, c ^ QUAD) for c in range(blocks)]
    plane_one = [(c, ((c + QUAD) ^ QUAD) - QUAD) for c in range(QUAD, blocks - QUAD)]
    sibling = [(c, c ^ 1) for c in range(blocks)]
    corners = [(c, c + REACH) for c in range(QUAD - 1, blocks - REACH, QUAD)]
    corners += [(c, c - REACH) for c in range(2 * QUAD, blocks, QUAD)]
    norm_scale = (segments * BAND) ** (-0.5)
    white = spectra(traces[0])
    corner = lax.ppermute(white, "chan", corners)
    other = lax.ppermute(white, "seg", [(0, 1), (1, 0)])
    across = lax.ppermute(white, "chan", [(c, c ^ 2) for c in range(blocks)])
    diagonal = [(s * blocks + c, (1 - s) * blocks + (c ^ 2)) for s in range(segments) for c in range(blocks)]
    diagonal = lax.ppermute(white, ("seg", "chan"), diagonal)
    quad = assemble(white, other, across, diagonal)
    first = lax.ppermute(quad, "chan", plane_one)
    second = lax.ppermute(quad, "chan", plane_two)
    near, corner = lax.optimization_barrier((quad, corner))
    beside = lax.ppermute(near, "chan", sibling)
    rows, scale = lag_rows(near, partners, traces.shape[2], half, norm_scale)
    rows, corner = lax.optimization_barrier((rows, corner))
    corner_other = lax.ppermute(corner, "seg", [(0, 1), (1, 0)])
    out = correlate(near_kernel, [rows, scale, quad, beside])
    corner = jnp.concatenate([corner, corner_other], axis=1)
    first, second, out = lax.optimization_barrier((first, second, out))
    sib_first = lax.ppermute(first, "chan", sibling)
    sib_second = lax.ppermute(second, "chan", sibling)
    tiles = correlate(own_kernel, [rows, scale, first, second], tiles_only=True)
    out = correlate(sibling_kernel, [rows, scale, sib_first, sib_second, corner, tiles], out)
    return out.reshape(1, slots, LAGS, half * channels)


def solution(mesh):
    placed = (P("seg", "chan", None), P("chan", None))
    return jax.shard_map(
        local, mesh=mesh, in_specs=placed, out_specs=P("chan", None, None, "seg"), check_vma=False
    )
```

```python
import functools
import math

import jax
import jax.numpy as jnp
import numpy as np
from jax import lax
from jax.experimental import pallas as pl
from jax.experimental.pallas import tpu as pltpu
from jax.sharding import PartitionSpec as P

BAND = 256
BAND_LO = 16
LAG = 32
LAGS = 2 * LAG + 1
REACH = 5
QUAD = 4
SPECTRUM_VMEM = 55040 * 2**10
KERNEL_VMEM = 24 * 2**20

water_level = 0.5
epsilon = 1e-06


def split_table(samples, step):
    bins = np.arange(BAND) + BAND_LO
    angle = (np.arange(step)[:, None] * bins[None, :] % samples) * (2.0 * math.pi / samples)
    table = np.concatenate([np.cos(angle), -np.sin(angle)], axis=1).astype(np.float32)
    high = table.astype(jnp.bfloat16)
    low = (table - high.astype(np.float32)).astype(jnp.bfloat16)
    return np.stack([high, low])


def spectrum_kernel(step, traces_hbm, table_hbm, white_ref, traces, table, sems):
    channels = white_ref.shape[0]
    stretches = traces.shape[0] // channels
    group = stretches
    table_copy = pltpu.make_async_copy(table_hbm, table, sems.at[stretches])
    table_copy.start()
    copies = [
        pltpu.make_async_copy(
            traces_hbm.at[:, pl.ds(n * step, step)], traces.at[pl.ds(n * channels, channels)], sems.at[n]
        )
        for n in range(stretches)
    ]
    for copy in copies:
        copy.start()
    number = lax.broadcasted_iota(jnp.int32, (stretches, BAND), 0)
    bins = lax.broadcasted_iota(jnp.int32, (stretches, BAND), 1) + BAND_LO
    turn = lax.rem(number * bins, stretches).astype(jnp.float32) * (2.0 * math.pi / stretches)
    turn_cos, turn_sin = jnp.cos(turn), jnp.sin(turn)
    table_copy.wait()
    real = imag = None
    for start in range(0, stretches, group):
        for copy in copies[start : start + group]:
            copy.wait()
        part = traces[start * channels : (start + group) * channels]
        y = jnp.dot(part, table[0], preferred_element_type=jnp.float32)
        y = y + jnp.dot(part, table[1], preferred_element_type=jnp.float32)
        for n in range(group):
            y_real = y[n * channels : (n + 1) * channels, :BAND]
            y_imag = y[n * channels : (n + 1) * channels, BAND:]
            if start + n == 0:
                real, imag = y_real, y_imag
                continue
            cosine, sine = turn_cos[start + n : start + n + 1], turn_sin[start + n : start + n + 1]
            real = real + (y_real * cosine + y_imag * sine)
            imag = imag + (y_imag * cosine - y_real * sine)
    power = real * real + imag * imag
    level = jnp.mean(power, axis=1, keepdims=True)
    inverse = lax.rsqrt(power + water_level * level + epsilon)
    white_ref[:, :BAND] = (real * inverse).astype(jnp.bfloat16)
    white_ref[:, BAND:] = (imag * inverse).astype(jnp.bfloat16)


def spectra(traces):
    channels, samples = traces.shape
    step = 256
    table = split_table(samples, step)
    hbm = pl.BlockSpec(memory_space=pltpu.HBM)
    return pl.pallas_call(
        functools.partial(spectrum_kernel, step),
        out_shape=jax.ShapeDtypeStruct((channels, 2 * BAND), jnp.bfloat16),
        in_specs=[hbm] * 2,
        out_specs=pl.BlockSpec(memory_space=pltpu.VMEM),
        scratch_shapes=[
            pltpu.VMEM((samples // step * channels, step), traces.dtype),
            pltpu.VMEM(table.shape, jnp.bfloat16),
            pltpu.SemaphoreType.DMA((samples // step + 1,)),
        ],
        cost_estimate=pl.CostEstimate(flops=10**9, bytes_accessed=2**20, transcendentals=0),
        compiler_params=pltpu.CompilerParams(vmem_limit_bytes=SPECTRUM_VMEM),
    )(traces, jnp.asarray(table))


def quad_kernel(white_ref, other_ref, across_ref, diagonal_ref, quad_ref):
    half = white_ref.shape[1]
    quad_ref[0, :, :half] = white_ref[...]
    quad_ref[0, :, half:] = other_ref[...]
    quad_ref[1, :, :half] = across_ref[...]
    quad_ref[1, :, half:] = diagonal_ref[...]


def assemble(*quarters):
    channels, depth = quarters[0].shape
    vmem = pl.BlockSpec(memory_space=pltpu.VMEM)
    return pl.pallas_call(
        quad_kernel,
        out_shape=jax.ShapeDtypeStruct((2, channels, 2 * depth), quarters[0].dtype),
        in_specs=[vmem] * 4,
        out_specs=vmem,
        compiler_params=pltpu.CompilerParams(vmem_limit_bytes=2 * 2**20),
        cost_estimate=pl.CostEstimate(flops=10**9, bytes_accessed=2**19, transcendentals=0),
    )(*quarters)


def rows_kernel(samples, norm_scale, pair_ref, partners_ref, rows_ref, scale_ref, stage, own, lag_cos, lag_sin):
    slots = scale_ref.shape[0]
    slot = lax.broadcasted_iota(jnp.int32, (slots, slots), 0) == lax.broadcasted_iota(jnp.int32, (slots, slots), 1)
    factor = jnp.where(slot & (jnp.broadcast_to(partners_ref[...], (slots, slots)) >= 0), norm_scale, 0.0)
    scale_ref[...] = jnp.broadcast_to(jnp.sum(factor, axis=1, keepdims=True), scale_ref.shape)
    lag = lax.broadcasted_iota(jnp.int32, lag_cos.shape, 0)
    bins = lax.broadcasted_iota(jnp.int32, lag_cos.shape, 1) + BAND_LO
    angle = lax.rem((lag + (samples - LAG)) * bins, samples).astype(jnp.float32) * (2.0 * math.pi / samples)
    lag_cos[...] = jnp.cos(angle)
    lag_sin[...] = jnp.sin(angle)
    pairs = own.shape[1]
    first = pl.multiple_of(lax.axis_index("seg") * 2 * pairs, 2 * pairs)
    mine = pair_ref[0, pl.ds(first, 2 * pairs), :].astype(jnp.float32)
    for left in range(0, mine.shape[1], 128):
        stage[...] = mine[:, left : left + 128]
        for member in range(2):
            own[member, :, left : left + 128] = stage[pl.ds(member, pairs, stride=2), :]

    def turn(lag, carry):
        cosine, sine = lag_cos[pl.ds(lag, 1), :], lag_sin[pl.ds(lag, 1), :]
        at = pl.ds(pl.multiple_of(lag * pairs, pairs), pairs)
        for member in range(2):
            for left in range(0, own.shape[2], 2 * BAND):
                middle, right = left + BAND, left + 2 * BAND
                real, imag = own[member, :, left:middle], own[member, :, middle:right]
                rows_ref[member, at, left:middle] = (real * cosine - imag * sine).astype(jnp.bfloat16)
                rows_ref[member, at, middle:right] = (real * sine + imag * cosine).astype(jnp.bfloat16)
        return carry

    lax.fori_loop(0, LAGS, turn, 0, unroll=5)


def multiply(rows_ref, window, scale, tiles, done):
    members = len(scale)
    width = window.shape[0] // members
    lines = rows_ref.shape[1]
    bounds = [lines * cut // 13 // 16 * 16 for cut in (0, 6, 10)] + [lines]
    for number, (low, high) in enumerate(zip(bounds[:-1], bounds[1:])):
        even, odd = [
            lax.dot_general(
                rows_ref[m, low:high], window[...], (((1,), (1,)), ((), ())), preferred_element_type=jnp.float32
            )
            for m in range(2)
        ]
        lane = lax.broadcasted_iota(jnp.int32, (high - low, 2 * width), 1)
        for n in range(0, members, 2):
            a, b = even[:, n * width : (n + 2) * width], odd[:, n * width : (n + 2) * width]
            tiles[n, low:high] = jnp.where(lane < width, a, pltpu.roll(b, width, 1)) * scale[n]
            tiles[n + 1, low:high] = jnp.where(lane < width, pltpu.roll(a, width, 1), b) * scale[n + 1]
        done(number, low, high)


class Sender:
    def __init__(self, tiles, slots, out_ref, sems):
        self.tiles, self.slots, self.out_ref, self.sems = tiles, slots, out_ref, sems
        self.sent = []

    def send(self, number, low, high):
        for n, slot in enumerate(self.slots):
            copy = pltpu.make_async_copy(
                self.tiles.at[n, low:high],
                self.out_ref.at[slot, low:high],
                self.sems.at[number * len(self.slots) + n],
            )
            self.sent.append(copy)
            copy.start()

    def wait(self):
        for copy in self.sent:
            copy.wait()


def slot_of(plane, swap_x, swap_core):
    place = lax.rem(lax.axis_index("chan"), QUAD)
    step_x = 2 - 4 * lax.div(place, 2)
    step_core = 1 - 2 * lax.rem(place, 2)
    return REACH + QUAD * plane + swap_x * step_x + swap_core * step_core


def near_kernel(rows_ref, scale_ref, own_ref, sibling_ref, out_ref, window, tiles, sems):
    width = own_ref.shape[1]
    slots = []
    for core, ref in enumerate((own_ref, sibling_ref)):
        for x in range(2):
            n = len(slots)
            window[n * width : (n + 1) * width] = ref[x]
            slots.append(slot_of(0, x, core))
    scale = [scale_ref[pl.ds(slot, 1), :] for slot in slots]
    sender = Sender(tiles, slots, out_ref, sems)
    multiply(rows_ref, window, scale, tiles, sender.send)
    sender.wait()


def far_slots(core):
    chan = lax.axis_index("chan")
    place = lax.rem(chan, QUAD)
    ahead = 2 * lax.rem(lax.div(chan, QUAD), 2) - 1
    side = 1 - 2 * lax.div(place, 2)
    last = jnp.clip(slot_of(side, 1, core), 0, 2 * REACH)
    if core == 1:
        last = jnp.where(place == 0, 0, jnp.where(place == QUAD - 1, 2 * REACH, last))
    slots = [slot_of(ahead, 0, core), slot_of(-ahead, 0, core), slot_of(-side, 1, core), last]
    return slots, (place == 0) | (place == QUAD - 1)


def load_far(first_ref, second_ref, window):
    chan = lax.axis_index("chan")
    width = first_ref.shape[1]
    ahead = 2 * lax.rem(lax.div(chan, QUAD), 2) - 1
    side = 1 - 2 * lax.div(lax.rem(chan, QUAD), 2)
    place = jnp.where(ahead == side, 3, 2)
    window[:width] = first_ref[0]
    window[width : 2 * width] = second_ref[0]
    window[pl.ds(pl.multiple_of(place * width, width), width), :] = first_ref[1]
    window[pl.ds(pl.multiple_of((5 - place) * width, width), width), :] = second_ref[1]


def own_kernel(rows_ref, scale_ref, first_ref, second_ref, tiles_ref, window):
    slots, _ = far_slots(0)
    load_far(first_ref, second_ref, window)
    scale = [scale_ref[pl.ds(slot, 1), :] for slot in slots]
    multiply(rows_ref, window, scale, tiles_ref, lambda *stretch: None)


def sibling_kernel(rows_ref, scale_ref, first_ref, second_ref, corner_ref, own_tiles_ref, near_ref, out_ref, window, tiles,
                   sems, own_sems):
    del near_ref
    own_sender = Sender(own_tiles_ref, far_slots(0)[0][:3], out_ref, own_sems)
    own_sender.send(0, 0, own_tiles_ref.shape[1])
    slots, stands = far_slots(1)
    load_far(first_ref, second_ref, window)

    @pl.when(stands)
    def _():
        window[3 * first_ref.shape[1] :] = corner_ref[...]

    scale = [scale_ref[pl.ds(slot, 1), :] for slot in slots]
    sender = Sender(tiles, slots, out_ref, sems)
    multiply(rows_ref, window, scale, tiles, sender.send)
    own_sender.wait()
    sender.wait()


def lag_rows(quad, partners, samples, half, norm_scale):
    width, depth = quad.shape[1:]
    vmem = pl.BlockSpec(memory_space=pltpu.VMEM)
    return pl.pallas_call(
        functools.partial(rows_kernel, samples, norm_scale),
        out_shape=[
            jax.ShapeDtypeStruct((2, LAGS * half // 2, depth), jnp.bfloat16),
            jax.ShapeDtypeStruct((partners.shape[1], 2 * width), jnp.float32),
        ],
        in_specs=[vmem, vmem],
        out_specs=[vmem, vmem],
        scratch_shapes=[
            pltpu.VMEM((half, 128), jnp.float32),
            pltpu.VMEM((2, half // 2, depth), jnp.float32),
            pltpu.VMEM((LAGS, BAND), jnp.float32),
            pltpu.VMEM((LAGS, BAND), jnp.float32),
        ],
        compiler_params=pltpu.CompilerParams(vmem_limit_bytes=KERNEL_VMEM),
        cost_estimate=pl.CostEstimate(flops=5 * 10**9, bytes_accessed=2**20, transcendentals=0),
    )(quad, partners)


def correlate(kernel, operands, out=None, tiles_only=False):
    rows, scale, blobs = operands[:3]
    width, depth = blobs.shape[-2:]
    lines = rows.shape[1]
    vmem = pl.BlockSpec(memory_space=pltpu.VMEM)
    anywhere = pl.BlockSpec(memory_space=pl.ANY)
    extra = [] if out is None else [out]
    scratch = [pltpu.VMEM((QUAD * width, depth), jnp.bfloat16)]
    if not tiles_only:
        scratch += [pltpu.VMEM((QUAD, lines, 2 * width), jnp.float32), pltpu.SemaphoreType.DMA((3 * QUAD,))]
    if extra:
        scratch += [pltpu.SemaphoreType.DMA((QUAD,))]
    return pl.pallas_call(
        kernel,
        out_shape=jax.ShapeDtypeStruct((QUAD if tiles_only else scale.shape[0], lines, 2 * width), jnp.float32),
        in_specs=[vmem] * len(operands) + [anywhere] * len(extra),
        out_specs=vmem if tiles_only else anywhere,
        scratch_shapes=scratch,
        input_output_aliases={len(operands): 0} if extra else {},
        compiler_params=pltpu.CompilerParams(vmem_limit_bytes=KERNEL_VMEM),
        cost_estimate=pl.CostEstimate(
            flops=4 * lines * depth * QUAD * width, bytes_accessed=8 * QUAD * lines * width, transcendentals=0
        ),
    )(*operands, *extra)


def local(traces, partners):
    slots = partners.shape[1]
    segments = lax.axis_size("seg")
    blocks = lax.axis_size("chan")
    channels = traces.shape[1]
    half = channels // segments
    assert segments == 2 and blocks % QUAD == 0 and slots == 2 * REACH + 1
    plane_two = [(c, c ^ QUAD) for c in range(blocks)]
    plane_one = [(c, ((c + QUAD) ^ QUAD) - QUAD) for c in range(QUAD, blocks - QUAD)]
    sibling = [(c, c ^ 1) for c in range(blocks)]
    corners = [(c, c + REACH) for c in range(QUAD - 1, blocks - REACH, QUAD)]
    corners += [(c, c - REACH) for c in range(2 * QUAD, blocks, QUAD)]
    norm_scale = (segments * BAND) ** (-0.5)
    white = spectra(traces[0])
    corner = lax.ppermute(white, "chan", corners)
    other = lax.ppermute(white, "seg", [(0, 1), (1, 0)])
    across = lax.ppermute(white, "chan", [(c, c ^ 2) for c in range(blocks)])
    diagonal = [(s * blocks + c, (1 - s) * blocks + (c ^ 2)) for s in range(segments) for c in range(blocks)]
    diagonal = lax.ppermute(white, ("seg", "chan"), diagonal)
    quad = assemble(white, other, across, diagonal)
    first = lax.ppermute(quad, "chan", plane_one)
    second = lax.ppermute(quad, "chan", plane_two)
    near, corner = lax.optimization_barrier((quad, corner))
    corner_other = lax.ppermute(corner, "seg", [(0, 1), (1, 0)])
    beside = lax.ppermute(near, "chan", sibling)
    rows, scale = lag_rows(near, partners, traces.shape[2], half, norm_scale)
    out = correlate(near_kernel, [rows, scale, quad, beside])
    corner = jnp.concatenate([corner, corner_other], axis=1)
    first, second, out = lax.optimization_barrier((first, second, out))
    sib_first = lax.ppermute(first, "chan", sibling)
    sib_second = lax.ppermute(second, "chan", sibling)
    tiles = correlate(own_kernel, [rows, scale, first, second], tiles_only=True)
    out = correlate(sibling_kernel, [rows, scale, sib_first, sib_second, corner, tiles], out)
    return out.reshape(1, slots, LAGS, half * channels)


def solution(mesh):
    placed = (P("seg", "chan", None), P("chan", None))
    return jax.shard_map(
        local, mesh=mesh, in_specs=placed, out_specs=P("chan", None, None, "seg"), check_vma=False
    )
```

```python
import functools
import math

import jax
import jax.numpy as jnp
import numpy as np
from jax import lax
from jax.experimental import pallas as pl
from jax.experimental.pallas import tpu as pltpu
from jax.sharding import PartitionSpec as P

BAND = 256
BAND_LO = 16
LAG = 32
LAGS = 2 * LAG + 1
REACH = 5
QUAD = 4
SPECTRUM_VMEM = 55040 * 2**10
KERNEL_VMEM = 24 * 2**20

water_level = 0.5
epsilon = 1e-06


def split_table(samples, step):
    bins = np.arange(BAND) + BAND_LO
    angle = (np.arange(step)[:, None] * bins[None, :] % samples) * (2.0 * math.pi / samples)
    table = np.concatenate([np.cos(angle), -np.sin(angle)], axis=1).astype(np.float32)
    high = table.astype(jnp.bfloat16)
    low = (table - high.astype(np.float32)).astype(jnp.bfloat16)
    return np.stack([high, low])


def spectrum_kernel(step, traces_hbm, table_hbm, white_ref, traces, table, sems):
    channels = white_ref.shape[0]
    stretches = traces.shape[0] // channels
    group = stretches
    table_copy = pltpu.make_async_copy(table_hbm, table, sems.at[stretches])
    table_copy.start()
    copies = [
        pltpu.make_async_copy(
            traces_hbm.at[:, pl.ds(n * step, step)], traces.at[pl.ds(n * channels, channels)], sems.at[n]
        )
        for n in range(stretches)
    ]
    for copy in copies:
        copy.start()
    number = lax.broadcasted_iota(jnp.int32, (stretches, BAND), 0)
    bins = lax.broadcasted_iota(jnp.int32, (stretches, BAND), 1) + BAND_LO
    turn = lax.rem(number * bins, stretches).astype(jnp.float32) * (2.0 * math.pi / stretches)
    turn_cos, turn_sin = jnp.cos(turn), jnp.sin(turn)
    table_copy.wait()
    real = imag = None
    for start in range(0, stretches, group):
        for copy in copies[start : start + group]:
            copy.wait()
        part = traces[start * channels : (start + group) * channels]
        y = jnp.dot(part, table[0], preferred_element_type=jnp.float32)
        y = y + jnp.dot(part, table[1], preferred_element_type=jnp.float32)
        for n in range(group):
            y_real = y[n * channels : (n + 1) * channels, :BAND]
            y_imag = y[n * channels : (n + 1) * channels, BAND:]
            if start + n == 0:
                real, imag = y_real, y_imag
                continue
            cosine, sine = turn_cos[start + n : start + n + 1], turn_sin[start + n : start + n + 1]
            real = real + (y_real * cosine + y_imag * sine)
            imag = imag + (y_imag * cosine - y_real * sine)
    power = real * real + imag * imag
    level = jnp.mean(power, axis=1, keepdims=True)
    denom = jnp.sqrt(power + water_level * level + epsilon)
    white_ref[:, :BAND] = (real / denom).astype(jnp.bfloat16)
    white_ref[:, BAND:] = (imag / denom).astype(jnp.bfloat16)


def spectra(traces):
    channels, samples = traces.shape
    step = 256
    table = split_table(samples, step)
    hbm = pl.BlockSpec(memory_space=pltpu.HBM)
    return pl.pallas_call(
        functools.partial(spectrum_kernel, step),
        out_shape=jax.ShapeDtypeStruct((channels, 2 * BAND), jnp.bfloat16),
        in_specs=[hbm] * 2,
        out_specs=pl.BlockSpec(memory_space=pltpu.VMEM),
        scratch_shapes=[
            pltpu.VMEM((samples // step * channels, step), traces.dtype),
            pltpu.VMEM(table.shape, jnp.bfloat16),
            pltpu.SemaphoreType.DMA((samples // step + 1,)),
        ],
        cost_estimate=pl.CostEstimate(flops=10**9, bytes_accessed=2**20, transcendentals=0),
        compiler_params=pltpu.CompilerParams(vmem_limit_bytes=SPECTRUM_VMEM),
    )(traces, jnp.asarray(table))


def quad_kernel(white_ref, other_ref, across_ref, diagonal_ref, quad_ref):
    half = white_ref.shape[1]
    quad_ref[0, :, :half] = white_ref[...]
    quad_ref[0, :, half:] = other_ref[...]
    quad_ref[1, :, :half] = across_ref[...]
    quad_ref[1, :, half:] = diagonal_ref[...]


def assemble(*quarters):
    channels, depth = quarters[0].shape
    vmem = pl.BlockSpec(memory_space=pltpu.VMEM)
    return pl.pallas_call(
        quad_kernel,
        out_shape=jax.ShapeDtypeStruct((2, channels, 2 * depth), quarters[0].dtype),
        in_specs=[vmem] * 4,
        out_specs=vmem,
        compiler_params=pltpu.CompilerParams(vmem_limit_bytes=2 * 2**20),
        cost_estimate=pl.CostEstimate(flops=10**9, bytes_accessed=2**19, transcendentals=0),
    )(*quarters)


def rows_kernel(samples, norm_scale, pair_ref, partners_ref, rows_ref, scale_ref, stage, own, lag_cos, lag_sin):
    slots = scale_ref.shape[0]
    slot = lax.broadcasted_iota(jnp.int32, (slots, slots), 0) == lax.broadcasted_iota(jnp.int32, (slots, slots), 1)
    factor = jnp.where(slot & (jnp.broadcast_to(partners_ref[...], (slots, slots)) >= 0), norm_scale, 0.0)
    scale_ref[...] = jnp.broadcast_to(jnp.sum(factor, axis=1, keepdims=True), scale_ref.shape)
    lag = lax.broadcasted_iota(jnp.int32, lag_cos.shape, 0)
    bins = lax.broadcasted_iota(jnp.int32, lag_cos.shape, 1) + BAND_LO
    angle = lax.rem((lag + (samples - LAG)) * bins, samples).astype(jnp.float32) * (2.0 * math.pi / samples)
    lag_cos[...] = jnp.cos(angle)
    lag_sin[...] = jnp.sin(angle)
    pairs = own.shape[1]
    first = pl.multiple_of(lax.axis_index("seg") * 2 * pairs, 2 * pairs)
    mine = pair_ref[0, pl.ds(first, 2 * pairs), :].astype(jnp.float32)
    for left in range(0, mine.shape[1], 128):
        stage[...] = mine[:, left : left + 128]
        for member in range(2):
            own[member, :, left : left + 128] = stage[pl.ds(member, pairs, stride=2), :]

    def turn(lag, carry):
        cosine, sine = lag_cos[pl.ds(lag, 1), :], lag_sin[pl.ds(lag, 1), :]
        at = pl.ds(pl.multiple_of(lag * pairs, pairs), pairs)
        for member in range(2):
            for left in range(0, own.shape[2], 2 * BAND):
                middle, right = left + BAND, left + 2 * BAND
                real, imag = own[member, :, left:middle], own[member, :, middle:right]
                rows_ref[member, at, left:middle] = (real * cosine - imag * sine).astype(jnp.bfloat16)
                rows_ref[member, at, middle:right] = (real * sine + imag * cosine).astype(jnp.bfloat16)
        return carry

    lax.fori_loop(0, LAGS, turn, 0, unroll=13)


def multiply(rows_ref, window, scale, tiles, done):
    members = len(scale)
    width = window.shape[0] // members
    lines = rows_ref.shape[1]
    bounds = [lines * cut // 13 // 16 * 16 for cut in (0, 6, 10)] + [lines]
    for number, (low, high) in enumerate(zip(bounds[:-1], bounds[1:])):
        even, odd = [
            lax.dot_general(
                rows_ref[m, low:high], window[...], (((1,), (1,)), ((), ())), preferred_element_type=jnp.float32
            )
            for m in range(2)
        ]
        lane = lax.broadcasted_iota(jnp.int32, (high - low, 2 * width), 1)
        for n in range(0, members, 2):
            a, b = even[:, n * width : (n + 2) * width], odd[:, n * width : (n + 2) * width]
            tiles[n, low:high] = jnp.where(lane < width, a, pltpu.roll(b, width, 1)) * scale[n]
            tiles[n + 1, low:high] = jnp.where(lane < width, pltpu.roll(a, width, 1), b) * scale[n + 1]
        done(number, low, high)


class Sender:
    def __init__(self, tiles, slots, out_ref, sems):
        self.tiles, self.slots, self.out_ref, self.sems = tiles, slots, out_ref, sems
        self.sent = []

    def send(self, number, low, high):
        for n, slot in enumerate(self.slots):
            copy = pltpu.make_async_copy(
                self.tiles.at[n, low:high],
                self.out_ref.at[slot, low:high],
                self.sems.at[number * len(self.slots) + n],
            )
            self.sent.append(copy)
            copy.start()

    def wait(self):
        for copy in self.sent:
            copy.wait()


def slot_of(plane, swap_x, swap_core):
    place = lax.rem(lax.axis_index("chan"), QUAD)
    step_x = 2 - 4 * lax.div(place, 2)
    step_core = 1 - 2 * lax.rem(place, 2)
    return REACH + QUAD * plane + swap_x * step_x + swap_core * step_core


def near_kernel(rows_ref, scale_ref, own_ref, sibling_ref, out_ref, window, tiles, sems):
    width = own_ref.shape[1]
    slots = []
    for core, ref in enumerate((own_ref, sibling_ref)):
        for x in range(2):
            n = len(slots)
            window[n * width : (n + 1) * width] = ref[x]
            slots.append(slot_of(0, x, core))
    scale = [scale_ref[pl.ds(slot, 1), :] for slot in slots]
    sender = Sender(tiles, slots, out_ref, sems)
    multiply(rows_ref, window, scale, tiles, sender.send)
    sender.wait()


def far_slots(core):
    chan = lax.axis_index("chan")
    place = lax.rem(chan, QUAD)
    ahead = 2 * lax.rem(lax.div(chan, QUAD), 2) - 1
    side = 1 - 2 * lax.div(place, 2)
    last = jnp.clip(slot_of(side, 1, core), 0, 2 * REACH)
    if core == 1:
        last = jnp.where(place == 0, 0, jnp.where(place == QUAD - 1, 2 * REACH, last))
    slots = [slot_of(ahead, 0, core), slot_of(-ahead, 0, core), slot_of(-side, 1, core), last]
    return slots, (place == 0) | (place == QUAD - 1)


def load_far(first_ref, second_ref, window):
    chan = lax.axis_index("chan")
    width = first_ref.shape[1]
    ahead = 2 * lax.rem(lax.div(chan, QUAD), 2) - 1
    side = 1 - 2 * lax.div(lax.rem(chan, QUAD), 2)
    place = jnp.where(ahead == side, 3, 2)
    window[:width] = first_ref[0]
    window[width : 2 * width] = second_ref[0]
    window[pl.ds(pl.multiple_of(place * width, width), width), :] = first_ref[1]
    window[pl.ds(pl.multiple_of((5 - place) * width, width), width), :] = second_ref[1]


def own_kernel(rows_ref, scale_ref, first_ref, second_ref, tiles_ref, window):
    slots, _ = far_slots(0)
    load_far(first_ref, second_ref, window)
    scale = [scale_ref[pl.ds(slot, 1), :] for slot in slots]
    multiply(rows_ref, window, scale, tiles_ref, lambda *stretch: None)


def sibling_kernel(rows_ref, scale_ref, first_ref, second_ref, corner_ref, own_tiles_ref, near_ref, out_ref, window, tiles,
                   sems, own_sems):
    del near_ref
    own_sender = Sender(own_tiles_ref, far_slots(0)[0][:3], out_ref, own_sems)
    own_sender.send(0, 0, own_tiles_ref.shape[1])
    slots, stands = far_slots(1)
    load_far(first_ref, second_ref, window)

    @pl.when(stands)
    def _():
        window[3 * first_ref.shape[1] :] = corner_ref[...]

    scale = [scale_ref[pl.ds(slot, 1), :] for slot in slots]
    sender = Sender(tiles, slots, out_ref, sems)
    multiply(rows_ref, window, scale, tiles, sender.send)
    own_sender.wait()
    sender.wait()


def lag_rows(quad, partners, samples, half, norm_scale):
    width, depth = quad.shape[1:]
    vmem = pl.BlockSpec(memory_space=pltpu.VMEM)
    return pl.pallas_call(
        functools.partial(rows_kernel, samples, norm_scale),
        out_shape=[
            jax.ShapeDtypeStruct((2, LAGS * half // 2, depth), jnp.bfloat16),
            jax.ShapeDtypeStruct((partners.shape[1], 2 * width), jnp.float32),
        ],
        in_specs=[vmem, vmem],
        out_specs=[vmem, vmem],
        scratch_shapes=[
            pltpu.VMEM((half, 128), jnp.float32),
            pltpu.VMEM((2, half // 2, depth), jnp.float32),
            pltpu.VMEM((LAGS, BAND), jnp.float32),
            pltpu.VMEM((LAGS, BAND), jnp.float32),
        ],
        compiler_params=pltpu.CompilerParams(vmem_limit_bytes=KERNEL_VMEM),
        cost_estimate=pl.CostEstimate(flops=5 * 10**9, bytes_accessed=2**20, transcendentals=0),
    )(quad, partners)


def correlate(kernel, operands, out=None, tiles_only=False):
    rows, scale, blobs = operands[:3]
    width, depth = blobs.shape[-2:]
    lines = rows.shape[1]
    vmem = pl.BlockSpec(memory_space=pltpu.VMEM)
    anywhere = pl.BlockSpec(memory_space=pl.ANY)
    extra = [] if out is None else [out]
    scratch = [pltpu.VMEM((QUAD * width, depth), jnp.bfloat16)]
    if not tiles_only:
        scratch += [pltpu.VMEM((QUAD, lines, 2 * width), jnp.float32), pltpu.SemaphoreType.DMA((3 * QUAD,))]
    if extra:
        scratch += [pltpu.SemaphoreType.DMA((QUAD,))]
    return pl.pallas_call(
        kernel,
        out_shape=jax.ShapeDtypeStruct((QUAD if tiles_only else scale.shape[0], lines, 2 * width), jnp.float32),
        in_specs=[vmem] * len(operands) + [anywhere] * len(extra),
        out_specs=vmem if tiles_only else anywhere,
        scratch_shapes=scratch,
        input_output_aliases={len(operands): 0} if extra else {},
        compiler_params=pltpu.CompilerParams(vmem_limit_bytes=KERNEL_VMEM),
        cost_estimate=pl.CostEstimate(
            flops=4 * lines * depth * QUAD * width, bytes_accessed=8 * QUAD * lines * width, transcendentals=0
        ),
    )(*operands, *extra)


def local(traces, partners):
    slots = partners.shape[1]
    segments = lax.axis_size("seg")
    blocks = lax.axis_size("chan")
    channels = traces.shape[1]
    half = channels // segments
    assert segments == 2 and blocks % QUAD == 0 and slots == 2 * REACH + 1
    plane_two = [(c, c ^ QUAD) for c in range(blocks)]
    plane_one = [(c, ((c + QUAD) ^ QUAD) - QUAD) for c in range(QUAD, blocks - QUAD)]
    sibling = [(c, c ^ 1) for c in range(blocks)]
    corners = [(c, c + REACH) for c in range(QUAD - 1, blocks - REACH, QUAD)]
    corners += [(c, c - REACH) for c in range(2 * QUAD, blocks, QUAD)]
    norm_scale = (segments * BAND) ** (-0.5)
    white = spectra(traces[0])
    corner = lax.ppermute(white, "chan", corners)
    other = lax.ppermute(white, "seg", [(0, 1), (1, 0)])
    across = lax.ppermute(white, "chan", [(c, c ^ 2) for c in range(blocks)])
    diagonal = [(s * blocks + c, (1 - s) * blocks + (c ^ 2)) for s in range(segments) for c in range(blocks)]
    diagonal = lax.ppermute(white, ("seg", "chan"), diagonal)
    quad = assemble(white, other, across, diagonal)
    first = lax.ppermute(quad, "chan", plane_one)
    second = lax.ppermute(quad, "chan", plane_two)
    near, corner = lax.optimization_barrier((quad, corner))
    corner_other = lax.ppermute(corner, "seg", [(0, 1), (1, 0)])
    beside = lax.ppermute(near, "chan", sibling)
    rows, scale = lag_rows(near, partners, traces.shape[2], half, norm_scale)
    out = correlate(near_kernel, [rows, scale, quad, beside])
    corner = jnp.concatenate([corner, corner_other], axis=1)
    first, second, out = lax.optimization_barrier((first, second, out))
    sib_first = lax.ppermute(first, "chan", sibling)
    sib_second = lax.ppermute(second, "chan", sibling)
    tiles = correlate(own_kernel, [rows, scale, first, second], tiles_only=True)
    out = correlate(sibling_kernel, [rows, scale, sib_first, sib_second, corner, tiles], out)
    return out.reshape(1, slots, LAGS, half * channels)


def solution(mesh):
    placed = (P("seg", "chan", None), P("chan", None))
    return jax.shard_map(
        local, mesh=mesh, in_specs=placed, out_specs=P("chan", None, None, "seg"), check_vma=False
    )
```
